32 devices in a mesh: lat: 4 (over y, x), lon: 8 (over z, core).
Axes of the slice: x: 2, y: 2, z: 4, core: 2. Of those that a mesh axis runs over, the one named last changes fastest.
Arguments:
- field: bfloat16 [8, 48, 192, 192], P(None, 'lat', 'lon'), may hold values from -6 to 6
- a_norm_one: float32 [192], replicated, may hold values from 0.1 to 1.9
- a_project: bfloat16 [192, 576], replicated, may hold values from -0.4375 to 0.4375
- a_bias: float32 [6, 144, 144], replicated, may hold values from -4 to 240
- a_output: bfloat16 [192, 192], replicated, may hold values from -0.4375 to 0.4375
- a_norm_two: float32 [192], replicated, may hold values from 0.1 to 1.9
- a_raise: bfloat16 [192, 768], replicated, may hold values from -0.4375 to 0.4375
- a_lower: bfloat16 [768, 192], replicated, may hold values from -0.21875 to 0.21875
- merge_norm_gain: float32 [768], replicated, may hold values from 0.1 to 1.9
- merge_weight: bfloat16 [768, 384], replicated, may hold values from -0.21875 to 0.21875
- b_norm_one: float32 [384], replicated, may hold values from 0.1 to 1.9
- b_project: bfloat16 [384, 1152], replicated, may hold values from -0.3125 to 0.3125
- b_bias: float32 [12, 144, 144], replicated, may hold values from -4 to 240
- b_output: bfloat16 [384, 384], replicated, may hold values from -0.3125 to 0.3125
- b_norm_two: float32 [384], replicated, may hold values from 0.1 to 1.9
- b_raise: bfloat16 [384, 1536], replicated, may hold values from -0.3125 to 0.3125
- b_lower: bfloat16 [1536, 384], replicated, may hold values from -0.15625 to 0.15625
- up_first: bfloat16 [384, 768], replicated, may hold values from -0.3125 to 0.3125
- up_norm: float32 [192], replicated, may hold values from 0.1 to 1.9
- up_second: bfloat16 [192, 192], replicated, may hold values from -0.4375 to 0.4375
Outputs:
- fine: bfloat16 [8, 48, 192, 192], P(None, 'lat', 'lon')
The draws below stay inside these ranges and needn't reach their ends.
All inputs are finite; a program needn't handle non-finite values.
Results may differ from the reference program's by a relative error of at most 0.023.
Values may be sent and summed in bfloat16 or wider, within the bound.
A program may use at most 192 MiB of HBM per device.

```python
import math
import jax
import jax.numpy as jnp
from jax import lax

P_SIZE = 8
C = 192
WIN_P = 2
WIN_LAT = 6
WIN_LON = 12
WIN = 144
C2 = 384
HEADS = 6
HEADS2 = 12
FF = 768
FF2 = 1536
LAT = 48
LON = 192


def draw_a_bias(key, part):
    key = jax.random.fold_in(key, 11)
    return jax.random.truncated_normal(key, -4.0, 4.0, (HEADS, WIN, WIN), jnp.float32)


def draw_b_bias(key, part):
    key = jax.random.fold_in(key, 12)
    return jax.random.truncated_normal(key, -4.0, 4.0, (HEADS2, WIN, WIN), jnp.float32)


def level_of(key, shape, pieces, smallest, largest):
    level = 1.0
    for dim, blocks in pieces:
        draws = jax.random.uniform(jax.random.fold_in(jax.random.fold_in(key, 6), dim), (blocks,), jnp.float32, smallest / len(pieces), largest / len(pieces))
        level = level * jnp.repeat(jnp.exp(draws), shape[dim] // blocks).reshape((-1,) + (1,) * (len(shape) - 1 - dim))
    return level


def gaussian(rng, extent, spread, bound, cuts=(), kind=jnp.bfloat16):
    values = spread * jax.random.normal(rng, extent, jnp.float32)
    if cuts:
        values = values * level_of(rng, extent, cuts, -0.22, 0.18)
    return jnp.clip(values, -bound, bound).astype(kind)


def setup_inputs(seed: int = 0) -> dict:
    splits = jax.random.split(jax.random.key(seed), 21)
    field = gaussian(splits[0], (P_SIZE, LAT, LON, C), 1.0, 6.0, ((1, 4), (2, 8)))
    a_norm_one = jnp.clip(1.0 + 0.18 * jax.random.normal(splits[1], (C,), jnp.float32), 0.1, 1.9)
    a_project = gaussian(splits[2], (C, 3 * C), C ** -0.5, 0.4375)
    a_bias = draw_a_bias(jax.random.fold_in(splits[20], 71), 0)
    a_output = gaussian(splits[4], (C, C), C ** -0.5, 0.4375)
    a_norm_two = jnp.clip(1.0 + 0.18 * jax.random.normal(splits[5], (C,), jnp.float32), 0.1, 1.9)
    a_raise = gaussian(splits[6], (C, FF), C ** -0.5, 0.4375)
    a_lower = gaussian(splits[7], (FF, C), FF ** -0.5, 0.21875)
    merge_norm_gain = jnp.clip(1.0 + 0.18 * jax.random.normal(splits[8], (4 * C,), jnp.float32), 0.1, 1.9)
    merge_weight = gaussian(splits[9], (4 * C, C2), (4 * C) ** -0.5, 0.21875)
    b_norm_one = jnp.clip(1.0 + 0.18 * jax.random.normal(splits[10], (C2,), jnp.float32), 0.1, 1.9)
    b_project = gaussian(splits[11], (C2, 3 * C2), C2 ** -0.5, 0.3125)
    b_bias = draw_b_bias(jax.random.fold_in(splits[20], 71), 0)
    b_output = gaussian(splits[13], (C2, C2), C2 ** -0.5, 0.3125)
    b_norm_two = jnp.clip(1.0 + 0.18 * jax.random.normal(splits[14], (C2,), jnp.float32), 0.1, 1.9)
    b_raise = gaussian(splits[15], (C2, FF2), C2 ** -0.5, 0.3125)
    b_lower = gaussian(splits[16], (FF2, C2), FF2 ** -0.5, 0.15625)
    up_first = gaussian(splits[17], (C2, 4 * C), C2 ** -0.5, 0.3125)
    up_norm = jnp.clip(1.0 + 0.18 * jax.random.normal(splits[18], (C,), jnp.float32), 0.1, 1.9)
    up_second = gaussian(splits[19], (C, C), C ** -0.5, 0.4375)
    return {"field": field, "a_norm_one": a_norm_one, "a_project": a_project, "a_bias": a_bias, "a_output": a_output, "a_norm_two": a_norm_two, "a_raise": a_raise, "a_lower": a_lower, "merge_norm_gain": merge_norm_gain, "merge_weight": merge_weight, "b_norm_one": b_norm_one, "b_project": b_project, "b_bias": b_bias, "b_output": b_output, "b_norm_two": b_norm_two, "b_raise": b_raise, "b_lower": b_lower, "up_first": up_first, "up_norm": up_norm, "up_second": up_second}


EPS = 1e-05

def layer_norm(values, norm_gain):
    average = lax.optimization_barrier(jnp.mean(values, axis=-1, keepdims=True))
    centred = values - average
    variance = lax.optimization_barrier(jnp.mean(centred * centred, axis=-1, keepdims=True))
    return centred * lax.rsqrt(variance + EPS) * norm_gain.astype(jnp.float32)

def norm_project(block, norm_gain, weight_matrix):
    flat = block.reshape(-1, block.shape[-1]).astype(jnp.float32)
    normed = layer_norm(flat, norm_gain).astype(jnp.bfloat16)
    result = jnp.dot(normed, weight_matrix, preferred_element_type=jnp.float32).astype(jnp.bfloat16)
    return result.reshape(block.shape[:-1] + (weight_matrix.shape[1],))

def partition(grid):
    depth, height, breadth, features = grid.shape
    tiles = grid.reshape(depth // WIN_P, WIN_P, height // WIN_LAT, WIN_LAT, breadth // WIN_LON, WIN_LON, features)
    return tiles.transpose(0, 2, 4, 1, 3, 5, 6).reshape(-1, WIN_P * WIN_LAT * WIN_LON, features)

def assemble(tiles, depth, height, breadth):
    features = tiles.shape[-1]
    grid = tiles.reshape(depth // WIN_P, height // WIN_LAT, breadth // WIN_LON, WIN_P, WIN_LAT, WIN_LON, features)
    return grid.transpose(0, 3, 1, 4, 2, 5, 6).reshape(depth, height, breadth, features)

def regions(depth, height, breadth, lat_start, lat_total):
    level_edge = (jnp.arange(depth, dtype=jnp.int32) == depth - 1).astype(jnp.int32)
    lat_edge = (lat_start + jnp.arange(height, dtype=jnp.int32) >= lat_total - WIN_LAT // 2).astype(jnp.int32)
    grid = 2 * level_edge[:, None, None] + lat_edge[None, :, None] + jnp.zeros((1, 1, breadth), jnp.int32)
    return partition(grid[..., None])[..., 0]

def attend(tiles, region, bias):
    heads = bias.shape[0]
    count, size, triple = tiles.shape
    width = triple // 3
    split = tiles.reshape(count, size, 3, heads, width // heads).astype(jnp.float32)
    scores = jnp.einsum('wqhd,wkhd->whqk', split[:, :, 0], split[:, :, 1])
    scores = scores * (1.0 / math.sqrt(width // heads)) + bias[None].astype(jnp.float32)
    allowed = region[:, :, None] == region[:, None, :]
    scores = jnp.where(allowed[:, None], scores, -1e+30)
    highest = lax.optimization_barrier(jnp.max(scores, axis=-1, keepdims=True))
    raised = jnp.exp(scores - highest)
    weights = (raised / lax.optimization_barrier(jnp.sum(raised, axis=-1, keepdims=True))).astype(jnp.bfloat16)
    mixed = jnp.einsum('whqk,wkhd->wqhd', weights.astype(jnp.float32), split[:, :, 2])
    return mixed.astype(jnp.bfloat16).reshape(count, size, width)

def shifted_block(field, gain_one, weight_qkv, bias, weight_out, gain_two, weight_up, weight_down):
    depth, height, breadth, width = field.shape

    def project_level(level):
        return norm_project(level, gain_one, weight_qkv)
    projected = lax.map(project_level, field)
    moved = jnp.roll(projected, (-(WIN_P // 2), -(WIN_LAT // 2), -(WIN_LON // 2)), axis=(0, 1, 2))
    tiles = partition(moved)
    region = regions(depth, height, breadth, 0, height)
    groups = depth // WIN_P * (height // WIN_LAT)
    size = tiles.shape[1]
    tiles = tiles.reshape(groups, -1, size, tiles.shape[2])
    region = region.reshape(groups, -1, size)

    def attend_group(pair):
        return attend(pair[0], pair[1], bias)
    mixed = lax.map(attend_group, (tiles, region))
    mixed = assemble(mixed.reshape(-1, size, width), depth, height, breadth)
    mixed = jnp.roll(mixed, (WIN_P // 2, WIN_LAT // 2, WIN_LON // 2), axis=(0, 1, 2))

    def finish(pair):
        level, attended = pair
        flat = level.reshape(-1, width).astype(jnp.float32)
        after = flat + jnp.dot(attended.reshape(-1, width), weight_out, preferred_element_type=jnp.float32)
        after = after.astype(jnp.bfloat16)
        normed = layer_norm(after.astype(jnp.float32), gain_two).astype(jnp.bfloat16)
        hidden = jax.nn.gelu(jnp.dot(normed, weight_up, preferred_element_type=jnp.float32), approximate=False)
        hidden = hidden.astype(jnp.bfloat16)
        result = after.astype(jnp.float32) + jnp.dot(hidden, weight_down, preferred_element_type=jnp.float32)
        return result.astype(jnp.bfloat16).reshape(height, breadth, width)
    return lax.map(finish, (field, mixed))

def merge_patches(field, norm_gain, weight_matrix):
    depth, height, breadth, width = field.shape
    merged = field.reshape(depth, height // 2, 2, breadth // 2, 2, width).transpose(0, 1, 3, 2, 4, 5)
    merged = merged.reshape(depth, height // 2, breadth // 2, 4 * width)
    return norm_project(merged, norm_gain, weight_matrix)

def upsample(coarse_grid, skip_state, first, norm_gain, second):
    depth, height, breadth, width = skip_state.shape
    flat = coarse_grid.reshape(-1, coarse_grid.shape[-1])
    raised = jnp.dot(flat, first, preferred_element_type=jnp.float32).astype(jnp.bfloat16)
    raised = raised.reshape(depth, height // 2, breadth // 2, 2, 2, width).transpose(0, 1, 3, 2, 4, 5)
    raised = raised.reshape(-1, width).astype(jnp.float32)
    normed = layer_norm(raised, norm_gain).astype(jnp.bfloat16)
    total = skip_state.reshape(-1, width).astype(jnp.float32) + jnp.dot(normed, second, preferred_element_type=jnp.float32)
    return total.astype(jnp.bfloat16).reshape(depth, height, breadth, width)

def reference(field, a_norm_one, a_project, a_bias, a_output, a_norm_two, a_raise, a_lower, merge_norm_gain, merge_weight, b_norm_one, b_project, b_bias, b_output, b_norm_two, b_raise, b_lower, up_first, up_norm, up_second):
    skip_state = shifted_block(field, a_norm_one, a_project, a_bias, a_output, a_norm_two, a_raise, a_lower)
    coarse_grid = merge_patches(skip_state, merge_norm_gain, merge_weight)
    coarse_grid = shifted_block(coarse_grid, b_norm_one, b_project, b_bias, b_output, b_norm_two, b_raise, b_lower)
    return upsample(coarse_grid, skip_state, up_first, up_norm, up_second)
```

```python
import functools
import math

import jax
import jax.numpy as jnp
import numpy as np
from jax import lax
from jax.experimental import pallas as pl
from jax.experimental.pallas import tpu as pltpu
from jax.sharding import PartitionSpec as P

WIN_P = 2
WIN_LAT = 6
WIN_LON = 12
HALF_LAT = WIN_LAT // 2
HALF_LON = WIN_LON // 2
HEAD = 32
LANES = 128
EPS = 1e-05
EXCLUDED = -1e30
MESH = pl.DeviceIdType.MESH
BF16 = jnp.bfloat16
F32 = jnp.float32


def pad16(count):
    return -(-count // 16) * 16


class Grid:
    def __init__(self, rows, columns):
        self.rows, self.columns = rows, columns
        self.local = WIN_P * rows * columns
        self.windows = self.local // (WIN_P * WIN_LAT * WIN_LON)
        counts = [
            WIN_P * HALF_LAT * (columns - HALF_LON),
            WIN_P * (rows - HALF_LAT) * HALF_LON,
            WIN_P * HALF_LAT * HALF_LON,
        ]
        self.sizes = [pad16(count) for count in counts]
        self.starts = [0, self.sizes[0], self.sizes[0] + self.sizes[1]]
        self.halo = sum(self.sizes)

    def natural(self, level, row, column):
        return (level * self.rows + row) * self.columns + column

    def slot(self, level, row, column):
        wide = self.columns - HALF_LON
        tall = self.rows - HALF_LAT
        if row < HALF_LAT and column >= HALF_LON:
            return (level * HALF_LAT + row) * wide + column - HALF_LON
        if row >= HALF_LAT and column < HALF_LON:
            return self.starts[1] + (level * tall + row - HALF_LAT) * HALF_LON + column
        return self.starts[2] + (level * HALF_LAT + row) * HALF_LON + column

    def send(self):
        matrix = np.zeros((self.halo, self.local), np.float32)
        for level in range(WIN_P):
            for row in range(self.rows):
                for column in range(self.columns):
                    if row < HALF_LAT or column < HALF_LON:
                        matrix[self.slot(level, row, column), self.natural(level, row, column)] = 1
        return matrix

    def gather(self):
        own = np.zeros((self.local, self.local), np.float32)
        halo = np.zeros((self.local, self.halo), np.float32)
        index = 0
        for top in range(0, self.rows, WIN_LAT):
            for left in range(0, self.columns, WIN_LON):
                for level in range(WIN_P):
                    for row in range(top + HALF_LAT, top + HALF_LAT + WIN_LAT):
                        for column in range(left + HALF_LON, left + HALF_LON + WIN_LON):
                            if row < self.rows and column < self.columns:
                                own[index, self.natural(level, row, column)] = 1
                            else:
                                halo[index, self.slot_ahead(level, row, column)] = 1
                            index += 1
        return own, halo

    def slot_ahead(self, level, row, column):
        return self.slot(
            level,
            row - self.rows if row >= self.rows else row,
            column - self.columns if column >= self.columns else column,
        )

    def quarters(self):
        matrix = np.zeros((self.local, self.local), np.float32)
        index = 0
        for r in range(2):
            for t in range(2):
                for level in range(WIN_P):
                    for row in range(r, self.rows, 2):
                        for column in range(t, self.columns, 2):
                            matrix[index, self.natural(level, row, column)] = 1
                            index += 1
        return matrix


def dot(a, b):
    return jnp.dot(a, b, preferred_element_type=F32)


def pick(matrix, values):
    return dot(matrix, values).astype(BF16)


def layer_norm(values, gain):
    average = jnp.mean(values, axis=-1, keepdims=True)
    centred = values - average
    variance = jnp.mean(centred * centred, axis=-1, keepdims=True)
    return centred * lax.rsqrt(variance + EPS) * gain


def gelu(x):
    return 0.5 * x * (1.0 + lax.erf(x * math.sqrt(0.5)))


def attend(q_ref, k_ref, v_ref, out_ref, rows, bias_ref, mask):
    size = mask.shape[0]
    width = q_ref.shape[-1]
    for start in range(0, width, LANES):
        lanes = slice(start, min(start + LANES, width))
        span = lanes.stop - start
        heads = span // HEAD
        first = start // HEAD
        q = q_ref[rows, lanes]
        lane = lax.broadcasted_iota(jnp.int32, (size, span), 1) // HEAD
        stack = jnp.concatenate(
            [jnp.where(lane == head, q, jnp.zeros_like(q)) for head in range(heads)], axis=0
        )
        scores = lax.dot_general(
            stack, k_ref[rows, lanes], (((1,), (1,)), ((), ())), preferred_element_type=F32
        )
        scores = scores * (1.0 / math.sqrt(HEAD)) + bias_ref[first * size : (first + heads) * size, :]
        scores = (scores.reshape(heads, size, size) + mask[None]).reshape(heads * size, size)
        highest = jnp.max(scores, axis=-1, keepdims=True)
        raised = jnp.exp(scores - highest)
        total = jnp.sum(raised, axis=-1, keepdims=True)
        mixed = dot(raised.astype(BF16), v_ref[rows, lanes]) / total
        result = jnp.zeros((size, span), F32)
        for head in range(heads):
            result = jnp.where(lane == head, mixed[head * size : (head + 1) * size], result)
        out_ref[rows, lanes] = result.astype(BF16)


def feed_forward(after, gain, up_ref, down_ref):
    normed = layer_norm(after, gain).astype(BF16)
    total = after
    width = up_ref.shape[1]
    for start in range(0, width, 256):
        columns = slice(start, start + 256)
        hidden = gelu(dot(normed, up_ref[:, columns])).astype(BF16)
        total = total + dot(hidden, down_ref[columns, :])
    return total.astype(BF16)


def section(fine, coarse, lats, lons, *refs):
    (
        field, a_norm_one, a_project, a_bias, a_output, a_norm_two, a_raise, a_lower,
        merge_gain, merge_weight,
        b_norm_one, b_project, b_bias, b_output, b_norm_two, b_raise, b_lower,
        up_first, up_norm, up_second,
        fine_send, fine_own, fine_halo, fine_send_back, fine_own_back, fine_halo_back, quarter, quarter_back,
        coarse_send, coarse_own, coarse_halo, coarse_send_back, coarse_own_back, coarse_halo_back,
        level_mask, lat_mask,
        out,
        fine_normed, skip, coarse_in, coarse_normed, q_ref, k_ref, v_ref, attended, coarse_attended,
        qc_ref, kc_ref, vc_ref, parts,
        out_one, in_one, out_two, in_two, out_three, in_three, out_four, in_four,
        send_sems, recv_sems,
    ) = refs
    depth = field.shape[0]
    pairs = depth // WIN_P
    width = field.shape[2]
    size = WIN_P * WIN_LAT * WIN_LON
    level_size = field.shape[1]
    lat, lon = lax.axis_index("lat"), lax.axis_index("lon")
    lat_next, lat_last = lax.rem(lat + 1, lats), lax.rem(lat + lats - 1, lats)
    lon_next, lon_last = lax.rem(lon + 1, lons), lax.rem(lon + lons - 1, lons)
    behind = ((lat_last, lon), (lat, lon_last), (lat_last, lon_last))
    ahead = ((lat_next, lon), (lat, lon_next), (lat_next, lon_next))

    barrier = pltpu.get_barrier_semaphore()
    for device in behind + ahead:
        pl.semaphore_signal(barrier, inc=1, device_id=device, device_id_type=MESH)
    pl.semaphore_wait(barrier, 6)

    def copies(phase, pair, grid, source, target, devices):
        made = []
        for part in range(3):
            rows = pl.ds(grid.starts[part], grid.sizes[part])
            made.append(
                pltpu.make_async_remote_copy(
                    src_ref=source.at[pair, rows],
                    dst_ref=target.at[pair, rows],
                    send_sem=send_sems.at[phase, pair, part],
                    recv_sem=recv_sems.at[phase, pair, part],
                    device_id=devices[part],
                    device_id_type=MESH,
                )
            )
        return made

    phase_one = functools.partial(copies, 0, grid=fine, source=out_one, target=in_one, devices=behind)
    phase_two = functools.partial(copies, 1, grid=fine, source=out_two, target=in_two, devices=ahead)
    phase_three = functools.partial(copies, 2, grid=coarse, source=out_three, target=in_three, devices=behind)
    phase_four = functools.partial(copies, 3, grid=coarse, source=out_four, target=in_four, devices=ahead)

    def field_pair(pair):
        return jnp.concatenate([field[2 * pair + 1], field[lax.rem(2 * pair + 2, depth)]], axis=0)

    def level_flag(pair):
        return jnp.where(pair == pairs - 1, 1.0, 0.0).astype(F32)

    lat_flag = jnp.where(lat == lats - 1, 1.0, 0.0).astype(F32)

    def send_fine(pair, carry):
        normed = layer_norm(field_pair(pair).astype(F32), a_norm_one[...]).astype(BF16)
        fine_normed[pair] = normed
        out_one[pair] = pick(fine_send[...], normed)
        for copy in phase_one(pair):
            copy.start()
        return carry

    lax.fori_loop(0, pairs, send_fine, 0)

    project = a_project[...]
    for part in range(3):
        parts[part] = project[:, part * width : (part + 1) * width]

    def attend_fine(pair, carry):
        for copy in phase_one(pair):
            copy.wait_recv()
        tokens = (dot(fine_own[...], fine_normed[pair]) + dot(fine_halo[...], in_one[pair])).astype(BF16)
        for part, ref in enumerate((q_ref, k_ref, v_ref)):
            ref[...] = dot(tokens, parts[part]).astype(BF16)
        level = level_flag(pair) * level_mask[...]
        across = fine.columns // WIN_LON

        def window(index, inner):
            bottom = jnp.where(index >= fine.windows - across, lat_flag, 0.0)
            mask = level + bottom * lat_mask[...]
            rows = pl.ds(pl.multiple_of(index * size, size), size)
            attend(q_ref, k_ref, v_ref, attended.at[pair], rows, a_bias, mask)
            return inner

        lax.fori_loop(0, fine.windows, window, 0)
        out_two[pair] = pick(fine_send_back[...], attended[pair])
        for copy in phase_two(pair):
            copy.start()
        return carry

    lax.fori_loop(0, pairs, attend_fine, 0)

    def finish_fine(pair, carry):
        for copy in phase_two(pair):
            copy.wait_recv()
        mixed = (dot(fine_own_back[...], attended[pair]) + dot(fine_halo_back[...], in_two[pair])).astype(BF16)
        after = dot(quarter[...], field_pair(pair)) + dot(mixed, a_output[...])
        after = after.astype(BF16).astype(F32)
        state = feed_forward(after, a_norm_two[...], a_raise, a_lower)
        skip[pair] = state
        quarters = [state[i * size : (i + 1) * size].astype(F32) for i in range(4)]
        average = sum(jnp.sum(values, axis=-1, keepdims=True) for values in quarters) / (4 * width)
        centred = [values - average for values in quarters]
        variance = sum(jnp.sum(values * values, axis=-1, keepdims=True) for values in centred) / (4 * width)
        factor = lax.rsqrt(variance + EPS)
        merged = jnp.zeros((size, merge_weight.shape[1]), F32)
        for i in range(4):
            normed = (centred[i] * factor * merge_gain[i]).astype(BF16)
            merged = merged + dot(normed, merge_weight[i * width : (i + 1) * width, :])
        merged = merged.astype(BF16)
        coarse_in[pair] = merged
        normed = layer_norm(merged.astype(F32), b_norm_one[...]).astype(BF16)
        coarse_normed[pair] = normed
        out_three[pair] = pick(coarse_send[...], normed)
        for copy in phase_three(pair):
            copy.start()
        return carry

    lax.fori_loop(0, pairs, finish_fine, 0)

    def attend_coarse(pair, carry):
        for copy in phase_three(pair):
            copy.wait_recv()
        tokens = (dot(coarse_own[...], coarse_normed[pair]) + dot(coarse_halo[...], in_three[pair])).astype(BF16)
        double = tokens.shape[1]
        for part, ref in enumerate((qc_ref, kc_ref, vc_ref)):
            ref[...] = dot(tokens, b_project[:, part * double : (part + 1) * double]).astype(BF16)
        mask = level_flag(pair) * level_mask[...] + lat_flag * lat_mask[...]
        attend(qc_ref, kc_ref, vc_ref, coarse_attended.at[pair], pl.ds(0, size), b_bias, mask)
        out_four[pair] = pick(coarse_send_back[...], coarse_attended[pair])
        for copy in phase_four(pair):
            copy.start()
        return carry

    lax.fori_loop(0, pairs, attend_coarse, 0)

    def finish_coarse(pair, carry):
        for copy in phase_four(pair):
            copy.wait_recv()
        mixed = (
            dot(coarse_own_back[...], coarse_attended[pair]) + dot(coarse_halo_back[...], in_four[pair])
        ).astype(BF16)
        after = coarse_in[pair].astype(F32) + dot(mixed, b_output[...])
        after = after.astype(BF16).astype(F32)
        state = feed_forward(after, b_norm_two[...], b_raise, b_lower)
        raised = dot(state, up_first[...]).astype(BF16).astype(F32)
        raised = jnp.concatenate([raised[:, i * width : (i + 1) * width] for i in range(4)], axis=0)
        normed = layer_norm(raised, up_norm[...]).astype(BF16)
        total = (skip[pair].astype(F32) + dot(normed, up_second[...])).astype(BF16)
        total = pick(quarter_back[...], total)
        out[2 * pair + 1] = total[:level_size]
        out[lax.rem(2 * pair + 2, depth)] = total[level_size:]
        return carry

    lax.fori_loop(0, pairs, finish_coarse, 0)

    def drain(pair, carry):
        for phase in (phase_one, phase_two, phase_three, phase_four):
            for copy in phase(pair):
                copy.wait_send()
        return carry

    lax.fori_loop(0, pairs, drain, 0)


def body(
    lats, lons, field,
    a_norm_one, a_project, a_bias, a_output, a_norm_two, a_raise, a_lower,
    merge_norm_gain, merge_weight,
    b_norm_one, b_project, b_bias, b_output, b_norm_two, b_raise, b_lower,
    up_first, up_norm, up_second,
):
    depth, rows, columns, width = field.shape
    double = merge_weight.shape[1]
    pairs = depth // WIN_P
    size = WIN_P * WIN_LAT * WIN_LON
    fine, coarse = Grid(rows, columns), Grid(rows // 2, columns // 2)
    quarter = fine.quarters()

    def one_hot(matrix):
        return jnp.asarray(matrix.astype(BF16))

    fine_own, fine_halo = fine.gather()
    coarse_own, coarse_halo = coarse.gather()
    orders = [
        fine.send(), fine_own, fine_halo, fine_halo.T, quarter @ fine_own.T, quarter @ fine.send().T,
        quarter, quarter.T,
        coarse.send(), coarse_own, coarse_halo, coarse_halo.T, coarse_own.T, coarse.send().T,
    ]
    token = np.arange(size)
    level = token // (WIN_LAT * WIN_LON)
    edge = (token // WIN_LON) % WIN_LAT >= WIN_LAT - HALF_LAT
    masks = [
        np.where(kind[:, None] != kind[None, :], EXCLUDED, 0.0).astype(np.float32) for kind in (level, edge)
    ]
    operands = [
        field.reshape(depth, rows * columns, width),
        a_norm_one.reshape(1, -1), a_project, a_bias.reshape(-1, size), a_output, a_norm_two.reshape(1, -1),
        a_raise, a_lower,
        merge_norm_gain.reshape(4, 1, width), merge_weight,
        b_norm_one.reshape(1, -1), b_project, b_bias.reshape(-1, size), b_output, b_norm_two.reshape(1, -1),
        b_raise, b_lower,
        up_first, up_norm.reshape(1, -1), up_second,
    ]
    operands += [one_hot(matrix) for matrix in orders] + [jnp.asarray(mask) for mask in masks]
    vmem = pl.BlockSpec(memory_space=pltpu.VMEM)
    result = pl.pallas_call(
        functools.partial(section, fine, coarse, lats, lons),
        out_shape=jax.ShapeDtypeStruct((depth, rows * columns, width), BF16),
        in_specs=[vmem] * len(operands),
        out_specs=vmem,
        scratch_shapes=[
            pltpu.VMEM((pairs, fine.local, width), BF16),
            pltpu.VMEM((pairs, fine.local, width), BF16),
            pltpu.VMEM((pairs, coarse.local, double), BF16),
            pltpu.VMEM((pairs, coarse.local, double), BF16),
            pltpu.VMEM((fine.local, width), BF16),
            pltpu.VMEM((fine.local, width), BF16),
            pltpu.VMEM((fine.local, width), BF16),
            pltpu.VMEM((pairs, fine.local, width), BF16),
            pltpu.VMEM((pairs, coarse.local, double), BF16),
            pltpu.VMEM((coarse.local, double), BF16),
            pltpu.VMEM((coarse.local, double), BF16),
            pltpu.VMEM((coarse.local, double), BF16),
            pltpu.VMEM((3, width, width), BF16),
        ]
        + [pltpu.VMEM((pairs, fine.halo, width), BF16)] * 4
        + [pltpu.VMEM((pairs, coarse.halo, double), BF16)] * 4
        + [pltpu.SemaphoreType.DMA((4, pairs, 3)), pltpu.SemaphoreType.DMA((4, pairs, 3))],
        compiler_params=pltpu.CompilerParams(
            collective_id=0, has_side_effects=True, vmem_limit_bytes=56 * 1024 * 1024
        ),
    )(*operands)
    return result.reshape(field.shape)


def solution(mesh):
    in_specs = (P(None, "lat", "lon", None),) + (P(),) * 19
    return jax.shard_map(
        functools.partial(body, mesh.shape["lat"], mesh.shape["lon"]),
        mesh=mesh,
        in_specs=in_specs,
        out_specs=P(None, "lat", "lon", None),
        check_vma=False,
    )
```

```python
import functools
import math

import jax
import jax.numpy as jnp
import numpy as np
from jax import lax
from jax.experimental import pallas as pl
from jax.experimental.pallas import tpu as pltpu
from jax.sharding import PartitionSpec as P

WIN_P = 2
WIN_LAT = 6
WIN_LON = 12
HALF_LAT = WIN_LAT // 2
HALF_LON = WIN_LON // 2
HEAD = 32
GROUP = 256
LOG2E = math.log2(math.e)
EPS = 1e-05
EXCLUDED = -1e30
MESH = pl.DeviceIdType.MESH
BF16 = jnp.bfloat16
F32 = jnp.float32


def pad16(count):
    return -(-count // 16) * 16


class Grid:
    def __init__(self, rows, columns):
        self.rows, self.columns = rows, columns
        self.local = WIN_P * rows * columns
        self.windows = self.local // (WIN_P * WIN_LAT * WIN_LON)
        counts = [
            WIN_P * HALF_LAT * (columns - HALF_LON),
            WIN_P * (rows - HALF_LAT) * HALF_LON,
            WIN_P * HALF_LAT * HALF_LON,
        ]
        self.sizes = [pad16(count) for count in counts]
        self.starts = [0, self.sizes[0], self.sizes[0] + self.sizes[1]]
        self.halo = sum(self.sizes)

    def natural(self, level, row, column):
        return (level * self.rows + row) * self.columns + column

    def slot(self, level, row, column):
        wide = self.columns - HALF_LON
        tall = self.rows - HALF_LAT
        if row < HALF_LAT and column >= HALF_LON:
            return (level * HALF_LAT + row) * wide + column - HALF_LON
        if row >= HALF_LAT and column < HALF_LON:
            return self.starts[1] + (level * tall + row - HALF_LAT) * HALF_LON + column
        return self.starts[2] + (level * HALF_LAT + row) * HALF_LON + column

    def send(self):
        matrix = np.zeros((self.halo, self.local), np.float32)
        for level in range(WIN_P):
            for row in range(self.rows):
                for column in range(self.columns):
                    if row < HALF_LAT or column < HALF_LON:
                        matrix[self.slot(level, row, column), self.natural(level, row, column)] = 1
        return matrix

    def gather(self):
        own = np.zeros((self.local, self.local), np.float32)
        halo = np.zeros((self.local, self.halo), np.float32)
        index = 0
        for top in range(0, self.rows, WIN_LAT):
            for left in range(0, self.columns, WIN_LON):
                for level in range(WIN_P):
                    for row in range(top + HALF_LAT, top + HALF_LAT + WIN_LAT):
                        for column in range(left + HALF_LON, left + HALF_LON + WIN_LON):
                            if row < self.rows and column < self.columns:
                                own[index, self.natural(level, row, column)] = 1
                            else:
                                halo[index, self.slot_ahead(level, row, column)] = 1
                            index += 1
        return own, halo

    def slot_ahead(self, level, row, column):
        return self.slot(
            level,
            row - self.rows if row >= self.rows else row,
            column - self.columns if column >= self.columns else column,
        )

    def quarters(self):
        matrix = np.zeros((self.local, self.local), np.float32)
        index = 0
        for r in range(2):
            for t in range(2):
                for level in range(WIN_P):
                    for row in range(r, self.rows, 2):
                        for column in range(t, self.columns, 2):
                            matrix[index, self.natural(level, row, column)] = 1
                            index += 1
        return matrix


def dot(a, b):
    return jnp.dot(a, b, preferred_element_type=F32)


def across(a, b):
    return lax.dot_general(a, b, (((1,), (1,)), ((), ())), preferred_element_type=F32)


def pick(matrix, values):
    return dot(matrix, values).astype(BF16)


def layer_norm(values, gain):
    average = jnp.mean(values, axis=-1, keepdims=True)
    centred = values - average
    variance = jnp.mean(centred * centred, axis=-1, keepdims=True)
    return centred * lax.rsqrt(variance + EPS) * gain


def gelu(x):
    size = jnp.abs(x)
    below = 1.0 + (0.3275911 * math.sqrt(0.5)) * size
    t = pl.reciprocal(below, approx=True)
    t = t * (2.0 - below * t)
    tail = 0.5 * 1.061405429
    for term in (-1.453152027, 1.421413741, -0.284496736, 0.254829592):
        tail = tail * t + 0.5 * term
    return jnp.maximum(x, 0.0) - (size * t) * (tail * jnp.exp2((x * x) * (-0.5 * LOG2E)))


def attend(q_ref, k_ref, v_ref, out_ref, rows, bias_ref, fold_ref):
    size = fold_ref.shape[0]
    width = q_ref.shape[-1]
    for start in range(0, width, GROUP):
        lanes = slice(start, min(start + GROUP, width))
        span = lanes.stop - start
        heads = span // HEAD
        spot = start // HEAD * size
        q = q_ref[rows, lanes]
        lane = lax.broadcasted_iota(jnp.int32, (1, span), 1) // HEAD
        stack = jnp.concatenate([q * (lane == head).astype(BF16) for head in range(heads)], axis=0)
        scores = across(k_ref[rows, lanes], stack)
        scores = scores * (LOG2E / math.sqrt(HEAD)) + bias_ref[:, spot : spot + heads * size]
        raised = jnp.exp2(scores - jnp.max(scores, axis=0, keepdims=True))
        factor = 1.0 / jnp.sum(raised, axis=0, keepdims=True)
        mixed = lax.dot_general(
            v_ref[rows, lanes], raised.astype(BF16), (((0,), (0,)), ((), ())), preferred_element_type=F32
        )
        owner = lax.broadcasted_iota(jnp.int32, (1, heads * size), 1) // size
        mixed = [
            (mixed[head * HEAD : (head + 1) * HEAD] * jnp.where(owner == head, factor, 0.0)).astype(BF16)
            for head in range(heads)
        ]
        mixed = jnp.concatenate(mixed, axis=0)
        out_ref[rows, lanes] = across(fold_ref[:, : heads * size], mixed).astype(BF16)


def score_tables(bias_ref, table_ref):
    size = bias_ref.shape[1]
    half = size // WIN_P
    bias = jnp.transpose(bias_ref[...]) * LOG2E
    key = lax.broadcasted_iota(jnp.int32, (size, 1), 0)
    query = lax.rem(lax.broadcasted_iota(jnp.int32, (1, bias.shape[1]), 1), size)

    def edge(token):
        return lax.rem(token, half) // (HALF_LAT * WIN_LON)

    by_level = jnp.where(key // half != query // half, EXCLUDED, 0.0)
    by_row = jnp.where(edge(key) != edge(query), EXCLUDED, 0.0)
    table_ref[0] = bias
    table_ref[1] = bias + by_row
    table_ref[2] = bias + by_level
    table_ref[3] = bias + by_row + by_level


def feed_forward(after, gain, up_ref, down):
    normed = layer_norm(after, gain).astype(BF16)
    total = after
    width = up_ref.shape[1]
    for start in range(0, width, 256):
        columns = slice(start, start + 256)
        hidden = gelu(dot(normed, up_ref[:, columns])).astype(BF16)
        total = total + down(hidden, columns)
    return total.astype(BF16)


def section(fine, coarse, lats, lons, *refs):
    (
        field, a_norm_one, a_project, a_bias, a_output, a_norm_two, a_raise, a_lower,
        merge_gain, merge_weight,
        b_norm_one, b_project, b_bias, b_output, b_norm_two, b_raise, b_lower,
        up_first, up_norm, up_second,
        fine_send, fine_own, fine_halo, fine_send_back, fine_own_back, fine_halo_back, quarter, quarter_back,
        coarse_send, coarse_own, coarse_halo, coarse_send_back, coarse_own_back, coarse_halo_back,
        fold,
        out,
        fine_normed, skip, coarse_in, coarse_normed, q_ref, k_ref, v_ref, attended, coarse_attended,
        qc_ref, kc_ref, vc_ref, parts, fine_table, coarse_table,
        out_one, in_one, out_two, in_two, out_three, in_three, out_four, in_four,
        send_sems, recv_sems,
    ) = refs
    depth = field.shape[0]
    pairs = depth // WIN_P
    width = field.shape[2]
    size = WIN_P * WIN_LAT * WIN_LON
    level_size = field.shape[1]
    lat, lon = lax.axis_index("lat"), lax.axis_index("lon")
    lat_next, lat_last = lax.rem(lat + 1, lats), lax.rem(lat + lats - 1, lats)
    lon_next, lon_last = lax.rem(lon + 1, lons), lax.rem(lon + lons - 1, lons)
    behind = ((lat_last, lon), (lat, lon_last), (lat_last, lon_last))
    ahead = ((lat_next, lon), (lat, lon_next), (lat_next, lon_next))

    barrier = pltpu.get_barrier_semaphore()
    for device in behind + ahead:
        pl.semaphore_signal(barrier, inc=1, device_id=device, device_id_type=MESH)
    pl.semaphore_wait(barrier, 6)

    def copies(phase, pair, grid, source, target, devices):
        made = []
        for part in range(3):
            rows = pl.ds(grid.starts[part], grid.sizes[part])
            made.append(
                pltpu.make_async_remote_copy(
                    src_ref=source.at[pair, rows],
                    dst_ref=target.at[pair, rows],
                    send_sem=send_sems.at[phase, pair, part],
                    recv_sem=recv_sems.at[phase, pair, part],
                    device_id=devices[part],
                    device_id_type=MESH,
                )
            )
        return made

    phase_one = functools.partial(copies, 0, grid=fine, source=out_one, target=in_one, devices=behind)
    phase_two = functools.partial(copies, 1, grid=fine, source=out_two, target=in_two, devices=ahead)
    phase_three = functools.partial(copies, 2, grid=coarse, source=out_three, target=in_three, devices=behind)
    phase_four = functools.partial(copies, 3, grid=coarse, source=out_four, target=in_four, devices=ahead)

    def field_pair(pair):
        return jnp.concatenate([field[2 * pair + 1], field[lax.rem(2 * pair + 2, depth)]], axis=0)

    def table(pair, bottom):
        return 2 * ((pair + 1) // pairs) + bottom * ((lat + 1) // lats)

    def send_fine(pair, carry):
        normed = layer_norm(field_pair(pair).astype(F32), a_norm_one[...]).astype(BF16)
        fine_normed[pair] = normed
        out_one[pair] = pick(fine_send[...], normed)
        for copy in phase_one(pair):
            copy.start()
        return carry

    lax.fori_loop(0, pairs, send_fine, 0)

    project = a_project[...]
    for part in range(3):
        parts[part] = project[:, part * width : (part + 1) * width]
    score_tables(a_bias, fine_table)
    score_tables(b_bias, coarse_table)

    def attend_fine(pair, carry):
        for copy in phase_one(pair):
            copy.wait_recv()
        tokens = (dot(fine_own[...], fine_normed[pair]) + dot(fine_halo[...], in_one[pair])).astype(BF16)
        for part, ref in enumerate((q_ref, k_ref, v_ref)):
            ref[...] = dot(tokens, parts[part]).astype(BF16)
        beside = fine.columns // WIN_LON
        tall = fine.windows // beside

        def window(index, inner):
            rows = pl.ds(pl.multiple_of(index * size, size), size)
            scores = fine_table.at[table(pair, (index // beside + 1) // tall)]
            attend(q_ref, k_ref, v_ref, attended.at[pair], rows, scores, fold)
            return inner

        lax.fori_loop(0, fine.windows, window, 0)
        out_two[pair] = pick(fine_send_back[...], attended[pair])
        for copy in phase_two(pair):
            copy.start()
        return carry

    lax.fori_loop(0, pairs, attend_fine, 0)

    def finish_fine(pair, carry):
        for copy in phase_two(pair):
            copy.wait_recv()
        mixed = (dot(fine_own_back[...], attended[pair]) + dot(fine_halo_back[...], in_two[pair])).astype(BF16)
        after = dot(quarter[...], field_pair(pair)) + dot(mixed, a_output[...])
        after = after.astype(BF16).astype(F32)
        state = feed_forward(
            after, a_norm_two[...], a_raise, lambda hidden, span: across(hidden, a_lower[:, span])
        )
        skip[pair] = state
        quarters = [state[i * size : (i + 1) * size].astype(F32) for i in range(4)]
        average = sum(jnp.sum(values, axis=-1, keepdims=True) for values in quarters) / (4 * width)
        centred = [values - average for values in quarters]
        variance = sum(jnp.sum(values * values, axis=-1, keepdims=True) for values in centred) / (4 * width)
        factor = lax.rsqrt(variance + EPS)
        merged = jnp.zeros((size, merge_weight.shape[1]), F32)
        gain = merge_gain[...].reshape(1, -1)
        for i in range(4):
            normed = (centred[i] * factor * gain[:, i * width : (i + 1) * width]).astype(BF16)
            merged = merged + dot(normed, merge_weight[i * width : (i + 1) * width, :])
        merged = merged.astype(BF16)
        coarse_in[pair] = merged
        normed = layer_norm(merged.astype(F32), b_norm_one[...]).astype(BF16)
        coarse_normed[pair] = normed
        out_three[pair] = pick(coarse_send[...], normed)
        for copy in phase_three(pair):
            copy.start()
        return carry

    lax.fori_loop(0, pairs, finish_fine, 0)

    def attend_coarse(pair, carry):
        for copy in phase_three(pair):
            copy.wait_recv()
        tokens = (dot(coarse_own[...], coarse_normed[pair]) + dot(coarse_halo[...], in_three[pair])).astype(BF16)
        double = tokens.shape[1]
        for part, ref in enumerate((qc_ref, kc_ref, vc_ref)):
            ref[...] = dot(tokens, b_project[:, part * double : (part + 1) * double]).astype(BF16)
        scores = coarse_table.at[table(pair, 1)]
        attend(qc_ref, kc_ref, vc_ref, coarse_attended.at[pair], pl.ds(0, size), scores, fold)
        out_four[pair] = pick(coarse_send_back[...], coarse_attended[pair])
        for copy in phase_four(pair):
            copy.start()
        return carry

    lax.fori_loop(0, pairs, attend_coarse, 0)

    def finish_coarse(pair, carry):
        for copy in phase_four(pair):
            copy.wait_recv()
        mixed = (
            dot(coarse_own_back[...], coarse_attended[pair]) + dot(coarse_halo_back[...], in_four[pair])
        ).astype(BF16)
        after = coarse_in[pair].astype(F32) + dot(mixed, b_output[...])
        after = after.astype(BF16).astype(F32)
        state = feed_forward(
            after, b_norm_two[...], b_raise, lambda hidden, span: dot(hidden, b_lower[span, :])
        )
        raised = dot(state, up_first[...]).astype(BF16).astype(F32)
        raised = jnp.concatenate([raised[:, i * width : (i + 1) * width] for i in range(4)], axis=0)
        normed = layer_norm(raised, up_norm[...]).astype(BF16)
        total = (skip[pair].astype(F32) + dot(normed, up_second[...])).astype(BF16)
        total = pick(quarter_back[...], total)
        out[2 * pair + 1] = total[:level_size]
        out[lax.rem(2 * pair + 2, depth)] = total[level_size:]
        return carry

    lax.fori_loop(0, pairs, finish_coarse, 0)

    def drain(pair, carry):
        for phase in (phase_one, phase_two, phase_three, phase_four):
            for copy in phase(pair):
                copy.wait_send()
        return carry

    lax.fori_loop(0, pairs, drain, 0)


def body(
    lats, lons, field,
    a_norm_one, a_project, a_bias, a_output, a_norm_two, a_raise, a_lower,
    merge_norm_gain, merge_weight,
    b_norm_one, b_project, b_bias, b_output, b_norm_two, b_raise, b_lower,
    up_first, up_norm, up_second,
):
    depth, rows, columns, width = field.shape
    double = merge_weight.shape[1]
    pairs = depth // WIN_P
    size = WIN_P * WIN_LAT * WIN_LON
    fine, coarse = Grid(rows, columns), Grid(rows // 2, columns // 2)
    quarter = fine.quarters()

    def one_hot(matrix):
        return jnp.asarray(matrix.astype(BF16))

    fine_own, fine_halo = fine.gather()
    coarse_own, coarse_halo = coarse.gather()
    orders = [
        fine.send(), fine_own, fine_halo, fine_halo.T, quarter @ fine_own.T, quarter @ fine.send().T,
        quarter, quarter.T,
        coarse.send(), coarse_own, coarse_halo, coarse_halo.T, coarse_own.T, coarse.send().T,
    ]
    fold = np.tile(np.eye(size, dtype=np.float32), (1, GROUP // HEAD))
    operands = [
        field.reshape(depth, rows * columns, width),
        a_norm_one, a_project, a_bias.reshape(-1, size), a_output, a_norm_two,
        a_raise, a_lower.T,
        merge_norm_gain, merge_weight,
        b_norm_one, b_project, b_bias.reshape(-1, size), b_output, b_norm_two,
        b_raise, b_lower,
        up_first, up_norm, up_second,
    ]
    operands += [one_hot(matrix) for matrix in orders + [fold]]
    vmem = pl.BlockSpec(memory_space=pltpu.VMEM)
    result = pl.pallas_call(
        functools.partial(section, fine, coarse, lats, lons),
        out_shape=jax.ShapeDtypeStruct((depth, rows * columns, width), BF16),
        in_specs=[vmem] * len(operands),
        out_specs=vmem,
        scratch_shapes=[
            pltpu.VMEM((pairs, fine.local, width), BF16),
            pltpu.VMEM((pairs, fine.local, width), BF16),
            pltpu.VMEM((pairs, coarse.local, double), BF16),
            pltpu.VMEM((pairs, coarse.local, double), BF16),
            pltpu.VMEM((fine.local, width), BF16),
            pltpu.VMEM((fine.local, width), BF16),
            pltpu.VMEM((fine.local, width), BF16),
            pltpu.VMEM((pairs, fine.local, width), BF16),
            pltpu.VMEM((pairs, coarse.local, double), BF16),
            pltpu.VMEM((coarse.local, double), BF16),
            pltpu.VMEM((coarse.local, double), BF16),
            pltpu.VMEM((coarse.local, double), BF16),
            pltpu.VMEM((3, width, width), BF16),
            pltpu.VMEM((4, size, a_bias.shape[0] * size), F32),
            pltpu.VMEM((4, size, b_bias.shape[0] * size), F32),
        ]
        + [pltpu.VMEM((pairs, fine.halo, width), BF16)] * 4
        + [pltpu.VMEM((pairs, coarse.halo, double), BF16)] * 4
        + [pltpu.SemaphoreType.DMA((4, pairs, 3)), pltpu.SemaphoreType.DMA((4, pairs, 3))],
        compiler_params=pltpu.CompilerParams(
            collective_id=0, has_side_effects=True, vmem_limit_bytes=56 * 1024 * 1024
        ),
    )(*operands)
    return result.reshape(field.shape)


def solution(mesh):
    in_specs = (P(None, "lat", "lon", None),) + (P(),) * 19
    return jax.shard_map(
        functools.partial(body, mesh.shape["lat"], mesh.shape["lon"]),
        mesh=mesh,
        in_specs=in_specs,
        out_specs=P(None, "lat", "lon", None),
        check_vma=False,
    )
```

```python
import functools
import math

import jax
import jax.numpy as jnp
import numpy as np
from jax import lax
from jax.experimental import pallas as pl
from jax.experimental.pallas import tpu as pltpu
from jax.sharding import PartitionSpec as P

WIN_P = 2
WIN_LAT = 6
WIN_LON = 12
HALF_LAT = WIN_LAT // 2
HALF_LON = WIN_LON // 2
HEAD = 32
GROUP = 128
LOG2E = math.log2(math.e)
EPS = 1e-05
EXCLUDED = -1e30
EARLY = 5
MESH = pl.DeviceIdType.MESH
BF16 = jnp.bfloat16
F32 = jnp.float32


def pad16(count):
    return -(-count // 16) * 16


class Grid:
    def __init__(self, rows, columns):
        self.rows, self.columns = rows, columns
        self.local = WIN_P * rows * columns
        self.windows = self.local // (WIN_P * WIN_LAT * WIN_LON)
        counts = [
            WIN_P * HALF_LAT * (columns - HALF_LON),
            WIN_P * (rows - HALF_LAT) * HALF_LON,
            WIN_P * HALF_LAT * HALF_LON,
        ]
        self.sizes = [pad16(count) for count in counts]
        self.starts = [0, self.sizes[0], self.sizes[0] + self.sizes[1]]
        self.halo = sum(self.sizes)

    def natural(self, level, row, column):
        return (level * self.rows + row) * self.columns + column

    def slot(self, level, row, column):
        wide = self.columns - HALF_LON
        tall = self.rows - HALF_LAT
        if row < HALF_LAT and column >= HALF_LON:
            return (level * HALF_LAT + row) * wide + column - HALF_LON
        if row >= HALF_LAT and column < HALF_LON:
            return self.starts[1] + (level * tall + row - HALF_LAT) * HALF_LON + column
        return self.starts[2] + (level * HALF_LAT + row) * HALF_LON + column

    def send(self):
        matrix = np.zeros((self.halo, self.local), np.float32)
        for level in range(WIN_P):
            for row in range(self.rows):
                for column in range(self.columns):
                    if row < HALF_LAT or column < HALF_LON:
                        matrix[self.slot(level, row, column), self.natural(level, row, column)] = 1
        return matrix

    def gather(self):
        own = np.zeros((self.local, self.local), np.float32)
        halo = np.zeros((self.local, self.halo), np.float32)
        index = 0
        for top in range(0, self.rows, WIN_LAT):
            for left in range(0, self.columns, WIN_LON):
                for level in range(WIN_P):
                    for row in range(top + HALF_LAT, top + HALF_LAT + WIN_LAT):
                        for column in range(left + HALF_LON, left + HALF_LON + WIN_LON):
                            if row < self.rows and column < self.columns:
                                own[index, self.natural(level, row, column)] = 1
                            else:
                                halo[index, self.slot_ahead(level, row, column)] = 1
                            index += 1
        return own, halo

    def slot_ahead(self, level, row, column):
        return self.slot(
            level,
            row - self.rows if row >= self.rows else row,
            column - self.columns if column >= self.columns else column,
        )

    def quarters(self):
        matrix = np.zeros((self.local, self.local), np.float32)
        index = 0
        for r in range(2):
            for t in range(2):
                for level in range(WIN_P):
                    for row in range(r, self.rows, 2):
                        for column in range(t, self.columns, 2):
                            matrix[index, self.natural(level, row, column)] = 1
                            index += 1
        return matrix


def dot(a, b):
    return jnp.dot(a, b, preferred_element_type=F32)


def across(a, b):
    return lax.dot_general(a, b, (((1,), (1,)), ((), ())), preferred_element_type=F32)


def pick(matrix, values):
    return dot(matrix, values).astype(BF16)


def layer_norm(values, gain):
    average = jnp.mean(values, axis=-1, keepdims=True)
    centred = values - average
    variance = jnp.mean(centred * centred, axis=-1, keepdims=True)
    return centred * lax.rsqrt(variance + EPS) * gain


def gelu(x):
    size = jnp.abs(x)
    below = 1.0 + (0.3275911 * math.sqrt(0.5)) * size
    t = pl.reciprocal(below, approx=True)
    t = t * (2.0 - below * t)
    tail = 0.5 * 1.061405429
    for term in (-1.453152027, 1.421413741, -0.284496736, 0.254829592):
        tail = tail * t + 0.5 * term
    return jnp.maximum(x, 0.0) - (size * t) * (tail * jnp.exp2((x * x) * (-0.5 * LOG2E)))


def attend(q_ref, k_ref, v_ref, out_ref, rows, bias_ref, query_code, key_code):
    size = query_code.shape[0]
    width = out_ref.shape[-1]
    for start in range(0, width, GROUP):
        span = min(GROUP, width - start)
        heads = span // HEAD
        first = start // HEAD
        lanes = slice(start, start + GROUP)
        q = q_ref[rows, lanes]
        lane = lax.broadcasted_iota(jnp.int32, (1, GROUP), 1) // HEAD
        stack = jnp.concatenate([q * (lane == head).astype(BF16) for head in range(heads)], axis=0)
        stack = jnp.concatenate([stack, jnp.concatenate([query_code] * heads, axis=0)], axis=1)
        scores = across(stack, jnp.concatenate([k_ref[rows, lanes], key_code], axis=1))
        scores = scores + bias_ref[first * size : (first + heads) * size, :]
        raised = jnp.exp2(scores - jnp.max(scores, axis=-1, keepdims=True)).astype(BF16)
        mixed = dot(raised, v_ref[rows, 2 * start : 2 * start + 2 * GROUP])
        total = mixed[:, GROUP:]
        factor = pl.reciprocal(total, approx=True)
        mixed = mixed[:, :GROUP] * (factor * (2.0 - total * factor))
        result = mixed[:size]
        for head in range(1, heads):
            result = jnp.where(lane == head, mixed[head * size : (head + 1) * size], result)
        out_ref[rows, start : start + span] = result[:, :span].astype(BF16)


def feed_forward(after, gain, up_ref, down):
    normed = layer_norm(after, gain).astype(BF16)
    total = after
    width = up_ref.shape[1]
    for start in range(0, width, 256):
        columns = slice(start, start + 256)
        hidden = gelu(dot(normed, up_ref[:, columns])).astype(BF16)
        total = total + down(hidden, columns)
    return total.astype(BF16)


def section(fine, coarse, lats, lons, places, *refs):
    count = places[0]
    moved = places[1:]
    operands = list(refs[:count])
    (
        out,
        fine_normed, skip, coarse_in, coarse_normed, q_ref, k_ref, v_ref, attended, coarse_attended,
        qc_ref, kc_ref, vc_ref, parts, fine_table, coarse_table,
        out_one, in_one, out_two, in_two, out_three, in_three, out_four, in_four,
        send_sems, recv_sems, load_sems,
    ) = refs[count : len(refs) - len(moved)]
    loads = []
    for slot, (place, held) in enumerate(zip(moved, refs[len(refs) - len(moved) :])):
        loads.append(pltpu.make_async_copy(operands[place], held, load_sems.at[slot]))
        loads[-1].start()
        operands[place] = held
    (
        field, a_norm_one, a_project, a_bias, a_output, a_norm_two, a_raise, a_lower,
        merge_gain, merge_weight,
        b_norm_one, b_project, b_bias, b_output, b_norm_two, b_raise, b_lower,
        up_first, up_norm, up_second,
        fine_send, fine_own, fine_halo, fine_send_back, fine_own_back, fine_halo_back, quarter, quarter_back,
        coarse_send, coarse_own, coarse_halo, coarse_send_back, coarse_own_back, coarse_halo_back,
        query_code, level_code, edge_code,
    ) = operands
    depth = field.shape[0]
    pairs = depth // WIN_P
    width = field.shape[2]
    size = WIN_P * WIN_LAT * WIN_LON
    level_size = field.shape[1]
    lat, lon = lax.axis_index("lat"), lax.axis_index("lon")
    lat_next, lat_last = lax.rem(lat + 1, lats), lax.rem(lat + lats - 1, lats)
    lon_next, lon_last = lax.rem(lon + 1, lons), lax.rem(lon + lons - 1, lons)
    behind = ((lat_last, lon), (lat, lon_last), (lat_last, lon_last))
    ahead = ((lat_next, lon), (lat, lon_next), (lat_next, lon_next))

    barrier = pltpu.get_barrier_semaphore()
    for device in behind + ahead:
        pl.semaphore_signal(barrier, inc=1, device_id=device, device_id_type=MESH)
    pl.semaphore_wait(barrier, 6)

    def copies(phase, pair, grid, source, target, devices):
        made = []
        for part in range(3):
            rows = pl.ds(grid.starts[part], grid.sizes[part])
            made.append(
                pltpu.make_async_remote_copy(
                    src_ref=source.at[pair, rows],
                    dst_ref=target.at[pair, rows],
                    send_sem=send_sems.at[phase, pair, part],
                    recv_sem=recv_sems.at[phase, pair, part],
                    device_id=devices[part],
                    device_id_type=MESH,
                )
            )
        return made

    phase_one = functools.partial(copies, 0, grid=fine, source=out_one, target=in_one, devices=behind)
    phase_two = functools.partial(copies, 1, grid=fine, source=out_two, target=in_two, devices=ahead)
    phase_three = functools.partial(copies, 2, grid=coarse, source=out_three, target=in_three, devices=behind)
    phase_four = functools.partial(copies, 3, grid=coarse, source=out_four, target=in_four, devices=ahead)

    def field_pair(pair):
        return jnp.concatenate([field[2 * pair + 1], field[lax.rem(2 * pair + 2, depth)]], axis=0)

    def key_code(pair, bottom):
        level = ((pair + 1) // pairs).astype(F32)
        edge = (bottom * ((lat + 1) // lats)).astype(F32)
        return (level * level_code[...] + edge * edge_code[...]).astype(BF16)

    def project(tokens, weights, out_refs):
        q_out, k_out, v_out = out_refs
        q_out[...] = (dot(tokens, weights(0)) * (LOG2E / math.sqrt(HEAD))).astype(BF16)
        k_out[...] = dot(tokens, weights(1)).astype(BF16)
        values = dot(tokens, weights(2)).astype(BF16)
        ones = jnp.ones((values.shape[0], GROUP), BF16)
        for start in range(0, values.shape[1], GROUP):
            v_out[:, 2 * start : 2 * start + GROUP] = values[:, start : start + GROUP]
            v_out[:, 2 * start + GROUP : 2 * start + 2 * GROUP] = ones

    def send_fine(pair, carry):
        normed = layer_norm(field_pair(pair).astype(F32), a_norm_one[...]).astype(BF16)
        fine_normed[pair] = normed
        out_one[pair] = pick(fine_send[...], normed)
        for copy in phase_one(pair):
            copy.start()
        return carry

    lax.fori_loop(0, pairs, send_fine, 0)

    for load in loads[:EARLY]:
        load.wait()
    parts[...] = jnp.zeros_like(parts)
    joined = a_project[...]
    for part in range(3):
        parts[part, :, :width] = joined[:, part * width : (part + 1) * width]
    fine_table[...] = a_bias[...] * LOG2E

    def attend_fine(pair, carry):
        for copy in phase_one(pair):
            copy.wait_recv()
        tokens = (dot(fine_own[...], fine_normed[pair]) + dot(fine_halo[...], in_one[pair])).astype(BF16)
        project(tokens, lambda part: parts[part], (q_ref, k_ref, v_ref))
        beside = fine.columns // WIN_LON
        tall = fine.windows // beside

        for index in range(fine.windows):
            code = key_code(pair, (index // beside + 1) // tall)
            rows = slice(index * size, (index + 1) * size)
            attend(q_ref, k_ref, v_ref, attended.at[pair], rows, fine_table, query_code[...], code)
        out_two[pair] = pick(fine_send_back[...], attended[pair])
        for copy in phase_two(pair):
            copy.start()
        return carry

    lax.fori_loop(0, pairs, attend_fine, 0)

    for load in loads[EARLY:]:
        load.wait()
    coarse_table[...] = b_bias[...] * LOG2E

    def finish_fine(pair, carry):
        for copy in phase_two(pair):
            copy.wait_recv()
        mixed = (dot(fine_own_back[...], attended[pair]) + dot(fine_halo_back[...], in_two[pair])).astype(BF16)
        after = dot(quarter[...], field_pair(pair)) + dot(mixed, a_output[...])
        after = after.astype(BF16).astype(F32)
        state = feed_forward(
            after, a_norm_two[...], a_raise, lambda hidden, span: across(hidden, a_lower[:, span])
        )
        skip[pair] = state
        quarters = [state[i * size : (i + 1) * size].astype(F32) for i in range(4)]
        average = sum(jnp.sum(values, axis=-1, keepdims=True) for values in quarters) / (4 * width)
        centred = [values - average for values in quarters]
        variance = sum(jnp.sum(values * values, axis=-1, keepdims=True) for values in centred) / (4 * width)
        factor = lax.rsqrt(variance + EPS)
        merged = jnp.zeros((size, merge_weight.shape[1]), F32)
        gain = merge_gain[...].reshape(1, -1)
        for i in range(4):
            normed = (centred[i] * factor * gain[:, i * width : (i + 1) * width]).astype(BF16)
            merged = merged + dot(normed, merge_weight[i * width : (i + 1) * width, :])
        merged = merged.astype(BF16)
        coarse_in[pair] = merged
        normed = layer_norm(merged.astype(F32), b_norm_one[...]).astype(BF16)
        coarse_normed[pair] = normed
        out_three[pair] = pick(coarse_send[...], normed)
        for copy in phase_three(pair):
            copy.start()
        return carry

    lax.fori_loop(0, pairs, finish_fine, 0)

    def attend_coarse(pair, carry):
        for copy in phase_three(pair):
            copy.wait_recv()
        tokens = (dot(coarse_own[...], coarse_normed[pair]) + dot(coarse_halo[...], in_three[pair])).astype(BF16)
        double = tokens.shape[1]
        weights = lambda part: b_project[:, part * double : (part + 1) * double]
        project(tokens, weights, (qc_ref, kc_ref, vc_ref))
        attend(
            qc_ref, kc_ref, vc_ref, coarse_attended.at[pair], slice(0, size), coarse_table, query_code[...],
            key_code(pair, 1),
        )
        out_four[pair] = pick(coarse_send_back[...], coarse_attended[pair])
        for copy in phase_four(pair):
            copy.start()
        return carry

    lax.fori_loop(0, pairs, attend_coarse, 0)

    def finish_coarse(pair, carry):
        for copy in phase_four(pair):
            copy.wait_recv()
        mixed = (
            dot(coarse_own_back[...], coarse_attended[pair]) + dot(coarse_halo_back[...], in_four[pair])
        ).astype(BF16)
        after = coarse_in[pair].astype(F32) + dot(mixed, b_output[...])
        after = after.astype(BF16).astype(F32)
        state = feed_forward(
            after, b_norm_two[...], b_raise, lambda hidden, span: dot(hidden, b_lower[span, :])
        )
        raised = dot(state, up_first[...]).astype(BF16).astype(F32)
        raised = jnp.concatenate([raised[:, i * width : (i + 1) * width] for i in range(4)], axis=0)
        normed = layer_norm(raised, up_norm[...]).astype(BF16)
        total = (skip[pair].astype(F32) + dot(normed, up_second[...])).astype(BF16)
        total = pick(quarter_back[...], total)
        out[2 * pair + 1] = total[:level_size]
        out[lax.rem(2 * pair + 2, depth)] = total[level_size:]
        return carry

    lax.fori_loop(0, pairs, finish_coarse, 0)

    def drain(pair, carry):
        for phase in (phase_one, phase_two, phase_three, phase_four):
            for copy in phase(pair):
                copy.wait_send()
        return carry

    lax.fori_loop(0, pairs, drain, 0)


def body(
    lats, lons, field,
    a_norm_one, a_project, a_bias, a_output, a_norm_two, a_raise, a_lower,
    merge_norm_gain, merge_weight,
    b_norm_one, b_project, b_bias, b_output, b_norm_two, b_raise, b_lower,
    up_first, up_norm, up_second,
):
    depth, rows, columns, width = field.shape
    double = merge_weight.shape[1]
    pairs = depth // WIN_P
    size = WIN_P * WIN_LAT * WIN_LON
    fine, coarse = Grid(rows, columns), Grid(rows // 2, columns // 2)
    quarter = fine.quarters()

    def one_hot(matrix):
        return jnp.asarray(matrix.astype(BF16))

    fine_own, fine_halo = fine.gather()
    coarse_own, coarse_halo = coarse.gather()
    orders = [
        fine.send(), fine_own, fine_halo, fine_halo.T, quarter @ fine_own.T, quarter @ fine.send().T,
        quarter, quarter.T,
        coarse.send(), coarse_own, coarse_halo, coarse_halo.T, coarse_own.T, coarse.send().T,
    ]
    token = np.arange(size)
    level = token // (WIN_LAT * WIN_LON)
    edge = (token // WIN_LON) % WIN_LAT // HALF_LAT
    codes = np.zeros((3, size, GROUP), np.float32)
    for kind, flags in enumerate((level, edge)):
        codes[0, :, 2 * kind], codes[0, :, 2 * kind + 1] = flags, 1 - flags
        codes[kind + 1, :, 2 * kind], codes[kind + 1, :, 2 * kind + 1] = (
            EXCLUDED * (1 - flags), EXCLUDED * flags
        )
    operands = [
        field.reshape(depth, rows * columns, width),
        a_norm_one, a_project, a_bias.reshape(-1, size), a_output, a_norm_two,
        a_raise, a_lower.T,
        merge_norm_gain, merge_weight,
        b_norm_one, b_project, b_bias.reshape(-1, size), b_output, b_norm_two,
        b_raise, b_lower,
        up_first, up_norm, up_second,
    ]
    operands += [one_hot(matrix) for matrix in orders + [codes[0]]] + [jnp.asarray(code) for code in codes[1:]]
    vmem = pl.BlockSpec(memory_space=pltpu.VMEM)
    specs = [vmem] * len(operands)
    moved = [2, 3, 21, 22, 23, 24, 25, 26, 4, 6, 7, 9, 28, 29, 30, 11, 12, 31, 32, 33, 13, 15, 16, 17, 19, 27]
    for place in moved:
        specs[place] = pl.BlockSpec(memory_space=pl.ANY)
    wide = pl.cdiv(width, GROUP) * GROUP
    result = pl.pallas_call(
        functools.partial(section, fine, coarse, lats, lons, [len(operands)] + moved),
        out_shape=jax.ShapeDtypeStruct((depth, rows * columns, width), BF16),
        in_specs=specs,
        out_specs=vmem,
        scratch_shapes=[
            pltpu.VMEM((pairs, fine.local, width), BF16),
            pltpu.VMEM((pairs, fine.local, width), BF16),
            pltpu.VMEM((pairs, coarse.local, double), BF16),
            pltpu.VMEM((pairs, coarse.local, double), BF16),
            pltpu.VMEM((fine.local, wide), BF16),
            pltpu.VMEM((fine.local, wide), BF16),
            pltpu.VMEM((fine.local, 2 * wide), BF16),
            pltpu.VMEM((pairs, fine.local, width), BF16),
            pltpu.VMEM((pairs, coarse.local, double), BF16),
            pltpu.VMEM((coarse.local, double), BF16),
            pltpu.VMEM((coarse.local, double), BF16),
            pltpu.VMEM((coarse.local, 2 * double), BF16),
            pltpu.VMEM((3, width, wide), BF16),
            pltpu.VMEM((a_bias.shape[0] * size, size), F32),
            pltpu.VMEM((b_bias.shape[0] * size, size), F32),
        ]
        + [pltpu.VMEM((pairs, fine.halo, width), BF16)] * 4
        + [pltpu.VMEM((pairs, coarse.halo, double), BF16)] * 4
        + [pltpu.SemaphoreType.DMA((4, pairs, 3)), pltpu.SemaphoreType.DMA((4, pairs, 3))]
        + [pltpu.SemaphoreType.DMA((len(moved),))]
        + [pltpu.VMEM(operands[place].shape, operands[place].dtype) for place in moved],
        compiler_params=pltpu.CompilerParams(
            collective_id=0, has_side_effects=True, vmem_limit_bytes=56 * 1024 * 1024
        ),
    )(*operands)
    return result.reshape(field.shape)


def solution(mesh):
    in_specs = (P(None, "lat", "lon", None),) + (P(),) * 19
    return jax.shard_map(
        functools.partial(body, mesh.shape["lat"], mesh.shape["lon"]),
        mesh=mesh,
        in_specs=in_specs,
        out_specs=P(None, "lat", "lon", None),
        check_vma=False,
    )
```

```python
import functools
import math

import jax
import jax.numpy as jnp
import numpy as np
from jax import lax
from jax.experimental import pallas as pl
from jax.experimental.pallas import tpu as pltpu
from jax.sharding import PartitionSpec as P

WIN_P = 2
WIN_LAT = 6
WIN_LON = 12
HALF_LAT = WIN_LAT // 2
HALF_LON = WIN_LON // 2
HEAD = 32
GROUP = 128
LOG2E = math.log2(math.e)
EPS = 1e-05
EXCLUDED = -1e30
EARLY = 5
TOGETHER = 2
MESH = pl.DeviceIdType.MESH
BF16 = jnp.bfloat16
F32 = jnp.float32


def pad16(count):
    return -(-count // 16) * 16


class Grid:
    def __init__(self, rows, columns):
        self.rows, self.columns = rows, columns
        self.local = WIN_P * rows * columns
        self.windows = self.local // (WIN_P * WIN_LAT * WIN_LON)
        counts = [
            WIN_P * HALF_LAT * (columns - HALF_LON),
            WIN_P * (rows - HALF_LAT) * HALF_LON,
            WIN_P * HALF_LAT * HALF_LON,
        ]
        self.sizes = [pad16(count) for count in counts]
        self.starts = [0, self.sizes[0], self.sizes[0] + self.sizes[1]]
        self.halo = sum(self.sizes)

    def natural(self, level, row, column):
        return (level * self.rows + row) * self.columns + column

    def slot(self, level, row, column):
        wide = self.columns - HALF_LON
        tall = self.rows - HALF_LAT
        if row < HALF_LAT and column >= HALF_LON:
            return (level * HALF_LAT + row) * wide + column - HALF_LON
        if row >= HALF_LAT and column < HALF_LON:
            return self.starts[1] + (level * tall + row - HALF_LAT) * HALF_LON + column
        return self.starts[2] + (level * HALF_LAT + row) * HALF_LON + column

    def send(self):
        matrix = np.zeros((self.halo, self.local), np.float32)
        for level in range(WIN_P):
            for row in range(self.rows):
                for column in range(self.columns):
                    if row < HALF_LAT or column < HALF_LON:
                        matrix[self.slot(level, row, column), self.natural(level, row, column)] = 1
        return matrix

    def gather(self):
        own = np.zeros((self.local, self.local), np.float32)
        halo = np.zeros((self.local, self.halo), np.float32)
        index = 0
        for top in range(0, self.rows, WIN_LAT):
            for left in range(0, self.columns, WIN_LON):
                for level in range(WIN_P):
                    for row in range(top + HALF_LAT, top + HALF_LAT + WIN_LAT):
                        for column in range(left + HALF_LON, left + HALF_LON + WIN_LON):
                            if row < self.rows and column < self.columns:
                                own[index, self.natural(level, row, column)] = 1
                            else:
                                halo[index, self.slot_ahead(level, row, column)] = 1
                            index += 1
        return own, halo

    def slot_ahead(self, level, row, column):
        return self.slot(
            level,
            row - self.rows if row >= self.rows else row,
            column - self.columns if column >= self.columns else column,
        )

    def quarters(self):
        matrix = np.zeros((self.local, self.local), np.float32)
        index = 0
        for r in range(2):
            for t in range(2):
                for level in range(WIN_P):
                    for row in range(r, self.rows, 2):
                        for column in range(t, self.columns, 2):
                            matrix[index, self.natural(level, row, column)] = 1
                            index += 1
        return matrix


def dot(a, b):
    return jnp.dot(a, b, preferred_element_type=F32)


def across(a, b):
    return lax.dot_general(a, b, (((1,), (1,)), ((), ())), preferred_element_type=F32)


def pick(matrix, values):
    return dot(matrix, values).astype(BF16)


def layer_norm(values, gain):
    average = jnp.mean(values, axis=-1, keepdims=True)
    centred = values - average
    variance = jnp.mean(centred * centred, axis=-1, keepdims=True)
    return centred * lax.rsqrt(variance + EPS) * gain


def gelu(x):
    size = jnp.abs(x)
    below = 1.0 + (0.3275911 * math.sqrt(0.5)) * size
    t = pl.reciprocal(below, approx=True)
    t = t * (2.0 - below * t)
    tail = 0.5 * 1.061405429
    for term in (-1.453152027, 1.421413741, -0.284496736, 0.254829592):
        tail = tail * t + 0.5 * term
    return jnp.maximum(x, 0.0) - (size * t) * (tail * jnp.exp2((x * x) * (-0.5 * LOG2E)))


def attend(q_ref, k_ref, v_ref, out_ref, rows, bias_ref, query_code, key_code):
    size = query_code.shape[0]
    width = out_ref.shape[-1]
    for start in range(0, width, GROUP):
        span = min(GROUP, width - start)
        heads = span // HEAD
        first = start // HEAD
        lanes = slice(start, start + GROUP)
        q = q_ref[rows, lanes]
        lane = lax.broadcasted_iota(jnp.int32, (1, GROUP), 1) // HEAD
        stack = jnp.concatenate([q * (lane == head).astype(BF16) for head in range(heads)], axis=0)
        stack = jnp.concatenate([stack, jnp.concatenate([query_code] * heads, axis=0)], axis=1)
        scores = across(stack, jnp.concatenate([k_ref[rows, lanes], key_code], axis=1))
        scores = scores + bias_ref[first * size : (first + heads) * size, :]
        raised = jnp.exp2(scores - jnp.max(scores, axis=-1, keepdims=True)).astype(BF16)
        mixed = dot(raised, v_ref[rows, 2 * start : 2 * start + 2 * GROUP])
        total = mixed[:, GROUP:]
        factor = pl.reciprocal(total, approx=True)
        mixed = mixed[:, :GROUP] * (factor * (2.0 - total * factor))
        result = mixed[:size]
        for head in range(1, heads):
            result = jnp.where(lane == head, mixed[head * size : (head + 1) * size], result)
        out_ref[rows, start : start + span] = result[:, :span].astype(BF16)


def feed_forward(after, gain, up_ref, down):
    normed = layer_norm(after, gain).astype(BF16)
    total = after
    width = up_ref.shape[1]
    for start in range(0, width, 256):
        columns = slice(start, start + 256)
        hidden = gelu(dot(normed, up_ref[:, columns])).astype(BF16)
        total = total + down(hidden, columns)
    return total.astype(BF16)


def section(fine, coarse, lats, lons, places, *refs):
    count = places[0]
    moved = places[1:]
    operands = list(refs[:count])
    (
        out,
        fine_normed, skip, coarse_in, coarse_normed, q_ref, k_ref, v_ref, attended, coarse_attended,
        qc_ref, kc_ref, vc_ref, coarse_both, parts, fine_table, coarse_table,
        out_one, in_one, out_two, in_two, out_three, in_three, out_four, in_four,
        send_sems, recv_sems, load_sems,
    ) = refs[count : len(refs) - len(moved)]
    loads = []
    for slot, (place, held) in enumerate(zip(moved, refs[len(refs) - len(moved) :])):
        loads.append(pltpu.make_async_copy(operands[place], held, load_sems.at[slot]))
        loads[-1].start()
        operands[place] = held
    (
        field, a_norm_one, a_project, a_bias, a_output, a_norm_two, a_raise, a_lower,
        merge_gain, merge_weight,
        b_norm_one, b_project, b_bias, b_output, b_norm_two, b_raise, b_lower,
        up_first, up_norm, up_second,
        fine_send, fine_own, fine_halo, fine_send_back, fine_own_back, fine_halo_back, quarter, quarter_back,
        coarse_send, coarse_own, coarse_halo, coarse_send_back, coarse_own_back, coarse_halo_back,
        query_code, level_code, edge_code,
    ) = operands
    depth = field.shape[0]
    pairs = depth // WIN_P
    width = field.shape[2]
    size = WIN_P * WIN_LAT * WIN_LON
    level_size = field.shape[1]
    lat, lon = lax.axis_index("lat"), lax.axis_index("lon")
    lat_next, lat_last = lax.rem(lat + 1, lats), lax.rem(lat + lats - 1, lats)
    lon_next, lon_last = lax.rem(lon + 1, lons), lax.rem(lon + lons - 1, lons)
    behind = ((lat_last, lon), (lat, lon_last), (lat_last, lon_last))
    ahead = ((lat_next, lon), (lat, lon_next), (lat_next, lon_next))

    barrier = pltpu.get_barrier_semaphore()
    for device in behind + ahead:
        pl.semaphore_signal(barrier, inc=1, device_id=device, device_id_type=MESH)
    pl.semaphore_wait(barrier, 6)

    def copies(phase, pair, grid, source, target, devices):
        made = []
        for part in range(3):
            rows = pl.ds(grid.starts[part], grid.sizes[part])
            made.append(
                pltpu.make_async_remote_copy(
                    src_ref=source.at[pair, rows],
                    dst_ref=target.at[pair, rows],
                    send_sem=send_sems.at[phase, pair, part],
                    recv_sem=recv_sems.at[phase, pair, part],
                    device_id=devices[part],
                    device_id_type=MESH,
                )
            )
        return made

    phase_one = functools.partial(copies, 0, grid=fine, source=out_one, target=in_one, devices=behind)
    phase_two = functools.partial(copies, 1, grid=fine, source=out_two, target=in_two, devices=ahead)
    phase_three = functools.partial(copies, 2, grid=coarse, source=out_three, target=in_three, devices=behind)
    phase_four = functools.partial(copies, 3, grid=coarse, source=out_four, target=in_four, devices=ahead)

    def field_pair(pair):
        return jnp.concatenate([field[2 * pair + 1], field[lax.rem(2 * pair + 2, depth)]], axis=0)

    def key_code(pair, bottom):
        level = ((pair + 1) // pairs).astype(F32)
        edge = (bottom * ((lat + 1) // lats)).astype(F32)
        return (level * level_code[...] + edge * edge_code[...]).astype(BF16)

    def project(tokens, weights, out_refs):
        q_out, k_out, v_out = out_refs
        q_out[...] = (dot(tokens, weights(0)) * (LOG2E / math.sqrt(HEAD))).astype(BF16)
        k_out[...] = dot(tokens, weights(1)).astype(BF16)
        values = dot(tokens, weights(2)).astype(BF16)
        ones = jnp.ones((values.shape[0], GROUP), BF16)
        for start in range(0, values.shape[1], GROUP):
            v_out[:, 2 * start : 2 * start + GROUP] = values[:, start : start + GROUP]
            v_out[:, 2 * start + GROUP : 2 * start + 2 * GROUP] = ones

    def send_fine(pair, carry):
        normed = layer_norm(field_pair(pair).astype(F32), a_norm_one[...]).astype(BF16)
        fine_normed[pair] = normed
        out_one[pair] = pick(fine_send[...], normed)
        for copy in phase_one(pair):
            copy.start()
        return carry

    lax.fori_loop(0, pairs, send_fine, 0)

    for load in loads[:EARLY]:
        load.wait()
    parts[...] = jnp.zeros_like(parts)
    joined = a_project[...]
    for part in range(3):
        parts[part, :, :width] = joined[:, part * width : (part + 1) * width]
    fine_table[...] = a_bias[...] * LOG2E

    def attend_fine(pair, carry):
        for copy in phase_one(pair):
            copy.wait_recv()
        tokens = (dot(fine_own[...], fine_normed[pair]) + dot(fine_halo[...], in_one[pair])).astype(BF16)
        project(tokens, lambda part: parts[part], (q_ref, k_ref, v_ref))
        beside = fine.columns // WIN_LON
        tall = fine.windows // beside

        for index in range(fine.windows):
            code = key_code(pair, (index // beside + 1) // tall)
            rows = slice(index * size, (index + 1) * size)
            attend(q_ref, k_ref, v_ref, attended.at[pair], rows, fine_table, query_code[...], code)
        out_two[pair] = pick(fine_send_back[...], attended[pair])
        for copy in phase_two(pair):
            copy.start()
        return carry

    lax.fori_loop(0, pairs, attend_fine, 0)

    for load in loads[EARLY:]:
        load.wait()
    coarse_table[...] = b_bias[...] * LOG2E

    def chosen(step):
        return [TOGETHER * step + each for each in range(TOGETHER)]

    def split(values):
        return [values[each * size : (each + 1) * size] for each in range(TOGETHER)]

    def join(values):
        return jnp.concatenate(values, axis=0)

    def finish_fine(step, carry):
        for pair in chosen(step):
            for copy in phase_two(pair):
                copy.wait_recv()
        states = []
        for pair in chosen(step):
            mixed = dot(fine_own_back[...], attended[pair]) + dot(fine_halo_back[...], in_two[pair])
            after = dot(quarter[...], field_pair(pair)) + dot(mixed.astype(BF16), a_output[...])
            after = after.astype(BF16).astype(F32)
            states.append(
                feed_forward(after, a_norm_two[...], a_raise, lambda hidden, span: across(hidden, a_lower[:, span]))
            )
            skip[pair] = states[-1]
        quarters = [
            join([state[i * size : (i + 1) * size] for state in states]).astype(F32) for i in range(4)
        ]
        average = sum(jnp.sum(values, axis=-1, keepdims=True) for values in quarters) / (4 * width)
        centred = [values - average for values in quarters]
        variance = sum(jnp.sum(values * values, axis=-1, keepdims=True) for values in centred) / (4 * width)
        factor = lax.rsqrt(variance + EPS)
        merged = jnp.zeros((TOGETHER * size, merge_weight.shape[1]), F32)
        gain = merge_gain[...].reshape(1, -1)
        for i in range(4):
            normed = (centred[i] * factor * gain[:, i * width : (i + 1) * width]).astype(BF16)
            merged = merged + dot(normed, merge_weight[i * width : (i + 1) * width, :])
        merged = merged.astype(BF16)
        normed = layer_norm(merged.astype(F32), b_norm_one[...]).astype(BF16)
        for pair, plain, ready in zip(chosen(step), split(merged), split(normed)):
            out_three[pair] = pick(coarse_send[...], ready)
            for copy in phase_three(pair):
                copy.start()
            coarse_in[pair] = plain
            coarse_normed[pair] = ready
        return carry

    lax.fori_loop(0, pairs // TOGETHER, finish_fine, 0)

    def attend_coarse(step, carry):
        for pair in chosen(step):
            for copy in phase_three(pair):
                copy.wait_recv()
        tokens = join(
            [
                dot(coarse_own[...], coarse_normed[pair]) + dot(coarse_halo[...], in_three[pair])
                for pair in chosen(step)
            ]
        ).astype(BF16)
        double = tokens.shape[1]
        weights = lambda part: b_project[:, part * double : (part + 1) * double]
        project(tokens, weights, (qc_ref, kc_ref, vc_ref))
        for each, pair in enumerate(chosen(step)):
            attend(
                qc_ref, kc_ref, vc_ref, coarse_both, slice(each * size, (each + 1) * size), coarse_table,
                query_code[...], key_code(pair, 1),
            )
        for each, pair in enumerate(chosen(step)):
            mixed = coarse_both[each * size : (each + 1) * size]
            out_four[pair] = pick(coarse_send_back[...], mixed)
            for copy in phase_four(pair):
                copy.start()
            coarse_attended[pair] = mixed
        return carry

    lax.fori_loop(0, pairs // TOGETHER, attend_coarse, 0)

    def finish_coarse(step, carry):
        for pair in chosen(step):
            for copy in phase_four(pair):
                copy.wait_recv()
        mixed = join(
            [
                dot(coarse_own_back[...], coarse_attended[pair]) + dot(coarse_halo_back[...], in_four[pair])
                for pair in chosen(step)
            ]
        ).astype(BF16)
        after = join([coarse_in[pair] for pair in chosen(step)]).astype(F32) + dot(mixed, b_output[...])
        after = after.astype(BF16).astype(F32)
        state = feed_forward(
            after, b_norm_two[...], b_raise, lambda hidden, span: dot(hidden, b_lower[span, :])
        )
        raised = dot(state, up_first[...]).astype(BF16).astype(F32)
        raised = join([raised[:, i * width : (i + 1) * width] for i in range(4)])
        normed = layer_norm(raised, up_norm[...]).astype(BF16)
        added = dot(normed, up_second[...])
        for each, pair in enumerate(chosen(step)):
            own = join(
                [added[(i * TOGETHER + each) * size : (i * TOGETHER + each + 1) * size] for i in range(4)]
            )
            total = pick(quarter_back[...], (skip[pair].astype(F32) + own).astype(BF16))
            out[2 * pair + 1] = total[:level_size]
            out[lax.rem(2 * pair + 2, depth)] = total[level_size:]
        return carry

    lax.fori_loop(0, pairs // TOGETHER, finish_coarse, 0)

    def drain(pair, carry):
        for phase in (phase_one, phase_two, phase_three, phase_four):
            for copy in phase(pair):
                copy.wait_send()
        return carry

    lax.fori_loop(0, pairs, drain, 0)


def body(
    lats, lons, field,
    a_norm_one, a_project, a_bias, a_output, a_norm_two, a_raise, a_lower,
    merge_norm_gain, merge_weight,
    b_norm_one, b_project, b_bias, b_output, b_norm_two, b_raise, b_lower,
    up_first, up_norm, up_second,
):
    depth, rows, columns, width = field.shape
    double = merge_weight.shape[1]
    pairs = depth // WIN_P
    size = WIN_P * WIN_LAT * WIN_LON
    fine, coarse = Grid(rows, columns), Grid(rows // 2, columns // 2)
    quarter = fine.quarters()

    def one_hot(matrix):
        return jnp.asarray(matrix.astype(BF16))

    fine_own, fine_halo = fine.gather()
    coarse_own, coarse_halo = coarse.gather()
    orders = [
        fine.send(), fine_own, fine_halo, fine_halo.T, quarter @ fine_own.T, quarter @ fine.send().T,
        quarter, quarter.T,
        coarse.send(), coarse_own, coarse_halo, coarse_halo.T, coarse_own.T, coarse.send().T,
    ]
    token = np.arange(size)
    level = token // (WIN_LAT * WIN_LON)
    edge = (token // WIN_LON) % WIN_LAT // HALF_LAT
    codes = np.zeros((3, size, GROUP), np.float32)
    for kind, flags in enumerate((level, edge)):
        codes[0, :, 2 * kind], codes[0, :, 2 * kind + 1] = flags, 1 - flags
        codes[kind + 1, :, 2 * kind], codes[kind + 1, :, 2 * kind + 1] = (
            EXCLUDED * (1 - flags), EXCLUDED * flags
        )
    operands = [
        field.reshape(depth, rows * columns, width),
        a_norm_one, a_project, a_bias.reshape(-1, size), a_output, a_norm_two,
        a_raise, a_lower.T,
        merge_norm_gain, merge_weight,
        b_norm_one, b_project, b_bias.reshape(-1, size), b_output, b_norm_two,
        b_raise, b_lower,
        up_first, up_norm, up_second,
    ]
    operands += [one_hot(matrix) for matrix in orders + [codes[0]]] + [jnp.asarray(code) for code in codes[1:]]
    vmem = pl.BlockSpec(memory_space=pltpu.VMEM)
    specs = [vmem] * len(operands)
    moved = [2, 3, 21, 22, 23, 24, 25, 26, 4, 6, 7, 9, 28, 29, 30, 11, 12, 31, 32, 33, 13, 15, 16, 17, 19, 27]
    for place in moved:
        specs[place] = pl.BlockSpec(memory_space=pl.ANY)
    wide = pl.cdiv(width, GROUP) * GROUP
    result = pl.pallas_call(
        functools.partial(section, fine, coarse, lats, lons, [len(operands)] + moved),
        out_shape=jax.ShapeDtypeStruct((depth, rows * columns, width), BF16),
        in_specs=specs,
        out_specs=vmem,
        scratch_shapes=[
            pltpu.VMEM((pairs, fine.local, width), BF16),
            pltpu.VMEM((pairs, fine.local, width), BF16),
            pltpu.VMEM((pairs, coarse.local, double), BF16),
            pltpu.VMEM((pairs, coarse.local, double), BF16),
            pltpu.VMEM((fine.local, wide), BF16),
            pltpu.VMEM((fine.local, wide), BF16),
            pltpu.VMEM((fine.local, 2 * wide), BF16),
            pltpu.VMEM((pairs, fine.local, width), BF16),
            pltpu.VMEM((pairs, coarse.local, double), BF16),
            pltpu.VMEM((TOGETHER * coarse.local, double), BF16),
            pltpu.VMEM((TOGETHER * coarse.local, double), BF16),
            pltpu.VMEM((TOGETHER * coarse.local, 2 * double), BF16),
            pltpu.VMEM((TOGETHER * coarse.local, double), BF16),
            pltpu.VMEM((3, width, wide), BF16),
            pltpu.VMEM((a_bias.shape[0] * size, size), F32),
            pltpu.VMEM((b_bias.shape[0] * size, size), F32),
        ]
        + [pltpu.VMEM((pairs, fine.halo, width), BF16)] * 4
        + [pltpu.VMEM((pairs, coarse.halo, double), BF16)] * 4
        + [pltpu.SemaphoreType.DMA((4, pairs, 3)), pltpu.SemaphoreType.DMA((4, pairs, 3))]
        + [pltpu.SemaphoreType.DMA((len(moved),))]
        + [pltpu.VMEM(operands[place].shape, operands[place].dtype) for place in moved],
        compiler_params=pltpu.CompilerParams(
            collective_id=0, has_side_effects=True, vmem_limit_bytes=56 * 1024 * 1024
        ),
    )(*operands)
    return result.reshape(field.shape)


def solution(mesh):
    in_specs = (P(None, "lat", "lon", None),) + (P(),) * 19
    return jax.shard_map(
        functools.partial(body, mesh.shape["lat"], mesh.shape["lon"]),
        mesh=mesh,
        in_specs=in_specs,
        out_specs=P(None, "lat", "lon", None),
        check_vma=False,
    )
```

```python
import functools
import math

import jax
import jax.numpy as jnp
import numpy as np
from jax import lax
from jax.experimental import pallas as pl
from jax.experimental.pallas import tpu as pltpu
from jax.sharding import PartitionSpec as P

WIN_P = 2
WIN_LAT = 6
WIN_LON = 12
HALF_LAT = WIN_LAT // 2
HALF_LON = WIN_LON // 2
HEAD = 32
GROUP = 128
LOG2E = math.log2(math.e)
EPS = 1e-05
EXCLUDED = -1e30
EARLY = 5
TOGETHER = 2
MESH = pl.DeviceIdType.MESH
BF16 = jnp.bfloat16
F32 = jnp.float32


def pad16(count):
    return -(-count // 16) * 16


class Grid:
    def __init__(self, rows, columns):
        self.rows, self.columns = rows, columns
        self.local = WIN_P * rows * columns
        self.windows = self.local // (WIN_P * WIN_LAT * WIN_LON)
        counts = [
            WIN_P * HALF_LAT * (columns - HALF_LON),
            WIN_P * (rows - HALF_LAT) * HALF_LON,
            WIN_P * HALF_LAT * HALF_LON,
        ]
        self.sizes = [pad16(count) for count in counts]
        self.starts = [0, self.sizes[0], self.sizes[0] + self.sizes[1]]
        self.halo = sum(self.sizes)

    def natural(self, level, row, column):
        return (level * self.rows + row) * self.columns + column

    def slot(self, level, row, column):
        wide = self.columns - HALF_LON
        tall = self.rows - HALF_LAT
        if row < HALF_LAT and column >= HALF_LON:
            return (level * HALF_LAT + row) * wide + column - HALF_LON
        if row >= HALF_LAT and column < HALF_LON:
            return self.starts[1] + (level * tall + row - HALF_LAT) * HALF_LON + column
        return self.starts[2] + (level * HALF_LAT + row) * HALF_LON + column

    def send(self):
        matrix = np.zeros((self.halo, self.local), np.float32)
        for level in range(WIN_P):
            for row in range(self.rows):
                for column in range(self.columns):
                    if row < HALF_LAT or column < HALF_LON:
                        matrix[self.slot(level, row, column), self.natural(level, row, column)] = 1
        return matrix

    def gather(self):
        own = np.zeros((self.local, self.local), np.float32)
        halo = np.zeros((self.local, self.halo), np.float32)
        index = 0
        for top in range(0, self.rows, WIN_LAT):
            for left in range(0, self.columns, WIN_LON):
                for level in range(WIN_P):
                    for row in range(top + HALF_LAT, top + HALF_LAT + WIN_LAT):
                        for column in range(left + HALF_LON, left + HALF_LON + WIN_LON):
                            if row < self.rows and column < self.columns:
                                own[index, self.natural(level, row, column)] = 1
                            else:
                                halo[index, self.slot_ahead(level, row, column)] = 1
                            index += 1
        return own, halo

    def slot_ahead(self, level, row, column):
        return self.slot(
            level,
            row - self.rows if row >= self.rows else row,
            column - self.columns if column >= self.columns else column,
        )

    def quarters(self):
        matrix = np.zeros((self.local, self.local), np.float32)
        index = 0
        for r in range(2):
            for t in range(2):
                for level in range(WIN_P):
                    for row in range(r, self.rows, 2):
                        for column in range(t, self.columns, 2):
                            matrix[index, self.natural(level, row, column)] = 1
                            index += 1
        return matrix


def dot(a, b):
    return jnp.dot(a, b, preferred_element_type=F32)


def across(a, b):
    return lax.dot_general(a, b, (((1,), (1,)), ((), ())), preferred_element_type=F32)


def pick(matrix, values):
    return dot(matrix, values).astype(BF16)


def layer_norm(values, gain):
    average = jnp.mean(values, axis=-1, keepdims=True)
    centred = values - average
    variance = jnp.mean(centred * centred, axis=-1, keepdims=True)
    return centred * lax.rsqrt(variance + EPS) * gain


def gelu(x):
    x = x.astype(BF16)

    def number(value):
        return jnp.asarray(value, BF16)

    size = jnp.abs(x)
    t = pl.reciprocal(number(1.0) + number(0.3275911 * math.sqrt(0.5)) * size, approx=True)
    tail = number(0.5 * 1.061405429)
    for term in (-1.453152027, 1.421413741, -0.284496736, 0.254829592):
        tail = tail * t + number(0.5 * term)
    return jnp.maximum(x, number(0.0)) - (size * t) * (tail * jnp.exp2((x * x) * number(-0.5 * LOG2E)))


def attend(q_ref, k_ref, v_ref, out_ref, rows, bias_ref, query_code, key_code):
    size = query_code.shape[0]
    width = out_ref.shape[-1]
    for start in range(0, width, GROUP):
        span = min(GROUP, width - start)
        heads = span // HEAD
        first = start // HEAD
        lanes = slice(start, start + GROUP)
        q = q_ref[rows, lanes]
        lane = lax.broadcasted_iota(jnp.int32, (1, GROUP), 1) // HEAD
        stack = jnp.concatenate([q * (lane == head).astype(BF16) for head in range(heads)], axis=0)
        stack = jnp.concatenate([stack, jnp.concatenate([query_code] * heads, axis=0)], axis=1)
        scores = across(stack, jnp.concatenate([k_ref[rows, lanes], key_code], axis=1))
        scores = scores + bias_ref[first * size : (first + heads) * size, :]
        raised = jnp.exp2(scores - jnp.max(scores, axis=-1, keepdims=True)).astype(BF16)
        mixed = dot(raised, v_ref[rows, 2 * start : 2 * start + 2 * GROUP])
        total = mixed[:, GROUP:]
        factor = pl.reciprocal(total, approx=True)
        mixed = mixed[:, :GROUP] * (factor * (2.0 - total * factor))
        result = mixed[:size]
        for head in range(1, heads):
            result = jnp.where(lane == head, mixed[head * size : (head + 1) * size], result)
        out_ref[rows, start : start + span] = result[:, :span].astype(BF16)


def feed_forward(after, gain, up_ref, down):
    normed = layer_norm(after, gain).astype(BF16)
    total = after
    width = up_ref.shape[1]
    for start in range(0, width, 256):
        columns = slice(start, start + 256)
        hidden = gelu(dot(normed, up_ref[:, columns]))
        total = total + down(hidden, columns)
    return total.astype(BF16)


def section(fine, coarse, lats, lons, places, *refs):
    count = places[0]
    moved = places[1:]
    operands = list(refs[:count])
    (
        out,
        fine_normed, skip, coarse_in, coarse_normed, q_ref, k_ref, v_ref, attended, coarse_attended,
        qc_ref, kc_ref, vc_ref, coarse_both, fine_both, parts, fine_table, coarse_table,
        out_one, in_one, out_two, in_two, out_three, in_three, out_four, in_four,
        send_sems, recv_sems, load_sems,
    ) = refs[count : len(refs) - len(moved)]
    loads = []
    for slot, (place, held) in enumerate(zip(moved, refs[len(refs) - len(moved) :])):
        loads.append(pltpu.make_async_copy(operands[place], held, load_sems.at[slot]))
        loads[-1].start()
        operands[place] = held
    (
        field, a_norm_one, a_project, a_bias, a_output, a_norm_two, a_raise, a_lower,
        merge_gain, merge_weight,
        b_norm_one, b_project, b_bias, b_output, b_norm_two, b_raise, b_lower,
        up_first, up_norm, up_second,
        fine_send, fine_own, fine_halo, fine_send_back, fine_own_back, fine_halo_back, quarter, quarter_back,
        coarse_send, coarse_own, coarse_halo, coarse_send_back, coarse_own_back, coarse_halo_back,
        query_code, level_code, edge_code,
    ) = operands
    depth = field.shape[0]
    pairs = depth // WIN_P
    width = field.shape[2]
    size = WIN_P * WIN_LAT * WIN_LON
    level_size = field.shape[1]
    lat, lon = lax.axis_index("lat"), lax.axis_index("lon")
    lat_next, lat_last = lax.rem(lat + 1, lats), lax.rem(lat + lats - 1, lats)
    lon_next, lon_last = lax.rem(lon + 1, lons), lax.rem(lon + lons - 1, lons)
    behind = ((lat_last, lon), (lat, lon_last), (lat_last, lon_last))
    ahead = ((lat_next, lon), (lat, lon_next), (lat_next, lon_next))

    barrier = pltpu.get_barrier_semaphore()
    for device in behind + ahead:
        pl.semaphore_signal(barrier, inc=1, device_id=device, device_id_type=MESH)
    pl.semaphore_wait(barrier, 6)

    def copies(phase, pair, grid, source, target, devices):
        made = []
        for part in range(3):
            rows = pl.ds(grid.starts[part], grid.sizes[part])
            made.append(
                pltpu.make_async_remote_copy(
                    src_ref=source.at[pair, rows],
                    dst_ref=target.at[pair, rows],
                    send_sem=send_sems.at[phase, pair, part],
                    recv_sem=recv_sems.at[phase, pair, part],
                    device_id=devices[part],
                    device_id_type=MESH,
                )
            )
        return made

    phase_one = functools.partial(copies, 0, grid=fine, source=out_one, target=in_one, devices=behind)
    phase_two = functools.partial(copies, 1, grid=fine, source=out_two, target=in_two, devices=ahead)
    phase_three = functools.partial(copies, 2, grid=coarse, source=out_three, target=in_three, devices=behind)
    phase_four = functools.partial(copies, 3, grid=coarse, source=out_four, target=in_four, devices=ahead)

    def field_pair(pair):
        return jnp.concatenate([field[2 * pair + 1], field[lax.rem(2 * pair + 2, depth)]], axis=0)

    def key_code(pair, bottom):
        level = ((pair + 1) // pairs).astype(F32)
        edge = (bottom * ((lat + 1) // lats)).astype(F32)
        return (level * level_code[...] + edge * edge_code[...]).astype(BF16)

    def project(tokens, weights, out_refs):
        q_out, k_out, v_out = out_refs
        q_out[...] = (dot(tokens, weights(0)) * (LOG2E / math.sqrt(HEAD))).astype(BF16)
        k_out[...] = dot(tokens, weights(1)).astype(BF16)
        values = dot(tokens, weights(2)).astype(BF16)
        ones = jnp.ones((values.shape[0], GROUP), BF16)
        for start in range(0, values.shape[1], GROUP):
            v_out[:, 2 * start : 2 * start + GROUP] = values[:, start : start + GROUP]
            v_out[:, 2 * start + GROUP : 2 * start + 2 * GROUP] = ones

    def send_fine(pair, carry):
        normed = layer_norm(field_pair(pair).astype(F32), a_norm_one[...]).astype(BF16)
        fine_normed[pair] = normed
        out_one[pair] = pick(fine_send[...], normed)
        for copy in phase_one(pair):
            copy.start()
        return carry

    lax.fori_loop(0, pairs, send_fine, 0)

    for load in loads[:EARLY]:
        load.wait()
    parts[...] = jnp.zeros_like(parts)
    joined = a_project[...]
    for part in range(3):
        parts[part, :, :width] = joined[:, part * width : (part + 1) * width]
    fine_table[...] = a_bias[...] * LOG2E

    def chosen(step):
        return [TOGETHER * step + each for each in range(TOGETHER)]

    def attend_fine(step, carry):
        for pair in chosen(step):
            for copy in phase_one(pair):
                copy.wait_recv()
        beside = fine.columns // WIN_LON
        tall = fine.windows // beside
        for each, pair in enumerate(chosen(step)):
            tokens = (dot(fine_own[...], fine_normed[pair]) + dot(fine_halo[...], in_one[pair])).astype(BF16)
            held = (q_ref.at[each], k_ref.at[each], v_ref.at[each])
            project(tokens, lambda part: parts[part], held)
            for index in range(fine.windows):
                code = key_code(pair, (index // beside + 1) // tall)
                rows = slice(index * size, (index + 1) * size)
                attend(*held, fine_both.at[each], rows, fine_table, query_code[...], code)
        for each, pair in enumerate(chosen(step)):
            mixed = fine_both[each]
            out_two[pair] = pick(fine_send_back[...], mixed)
            for copy in phase_two(pair):
                copy.start()
            attended[pair] = mixed
        return carry

    lax.fori_loop(0, pairs // TOGETHER, attend_fine, 0)

    for load in loads[EARLY:]:
        load.wait()
    coarse_table[...] = b_bias[...] * LOG2E

    def split(values):
        return [values[each * size : (each + 1) * size] for each in range(TOGETHER)]

    def join(values):
        return jnp.concatenate(values, axis=0)

    def finish_fine(step, carry):
        for pair in chosen(step):
            for copy in phase_two(pair):
                copy.wait_recv()
        states = []
        for pair in chosen(step):
            mixed = dot(fine_own_back[...], attended[pair]) + dot(fine_halo_back[...], in_two[pair])
            after = dot(quarter[...], field_pair(pair)) + dot(mixed.astype(BF16), a_output[...])
            after = after.astype(BF16).astype(F32)
            states.append(
                feed_forward(after, a_norm_two[...], a_raise, lambda hidden, span: across(hidden, a_lower[:, span]))
            )
            skip[pair] = states[-1]
        quarters = [
            join([state[i * size : (i + 1) * size] for state in states]).astype(F32) for i in range(4)
        ]
        average = sum(jnp.sum(values, axis=-1, keepdims=True) for values in quarters) / (4 * width)
        centred = [values - average for values in quarters]
        variance = sum(jnp.sum(values * values, axis=-1, keepdims=True) for values in centred) / (4 * width)
        factor = lax.rsqrt(variance + EPS)
        merged = jnp.zeros((TOGETHER * size, merge_weight.shape[1]), F32)
        gain = merge_gain[...].reshape(1, -1)
        for i in range(4):
            normed = (centred[i] * factor * gain[:, i * width : (i + 1) * width]).astype(BF16)
            merged = merged + dot(normed, merge_weight[i * width : (i + 1) * width, :])
        merged = merged.astype(BF16)
        normed = layer_norm(merged.astype(F32), b_norm_one[...]).astype(BF16)
        for pair, plain, ready in zip(chosen(step), split(merged), split(normed)):
            out_three[pair] = pick(coarse_send[...], ready)
            for copy in phase_three(pair):
                copy.start()
            coarse_in[pair] = plain
            coarse_normed[pair] = ready
        return carry

    lax.fori_loop(0, pairs // TOGETHER, finish_fine, 0)

    def attend_coarse(step, carry):
        for pair in chosen(step):
            for copy in phase_three(pair):
                copy.wait_recv()
        tokens = join(
            [
                dot(coarse_own[...], coarse_normed[pair]) + dot(coarse_halo[...], in_three[pair])
                for pair in chosen(step)
            ]
        ).astype(BF16)
        double = tokens.shape[1]
        weights = lambda part: b_project[:, part * double : (part + 1) * double]
        project(tokens, weights, (qc_ref, kc_ref, vc_ref))
        for each, pair in enumerate(chosen(step)):
            attend(
                qc_ref, kc_ref, vc_ref, coarse_both, slice(each * size, (each + 1) * size), coarse_table,
                query_code[...], key_code(pair, 1),
            )
        for each, pair in enumerate(chosen(step)):
            mixed = coarse_both[each * size : (each + 1) * size]
            out_four[pair] = pick(coarse_send_back[...], mixed)
            for copy in phase_four(pair):
                copy.start()
            coarse_attended[pair] = mixed
        return carry

    lax.fori_loop(0, pairs // TOGETHER, attend_coarse, 0)

    def finish_coarse(step, carry):
        for pair in chosen(step):
            for copy in phase_four(pair):
                copy.wait_recv()
        mixed = join(
            [
                dot(coarse_own_back[...], coarse_attended[pair]) + dot(coarse_halo_back[...], in_four[pair])
                for pair in chosen(step)
            ]
        ).astype(BF16)
        after = join([coarse_in[pair] for pair in chosen(step)]).astype(F32) + dot(mixed, b_output[...])
        after = after.astype(BF16).astype(F32)
        state = feed_forward(
            after, b_norm_two[...], b_raise, lambda hidden, span: dot(hidden, b_lower[span, :])
        )
        raised = dot(state, up_first[...]).astype(BF16).astype(F32)
        raised = join([raised[:, i * width : (i + 1) * width] for i in range(4)])
        normed = layer_norm(raised, up_norm[...]).astype(BF16)
        added = dot(normed, up_second[...])
        for each, pair in enumerate(chosen(step)):
            own = join(
                [added[(i * TOGETHER + each) * size : (i * TOGETHER + each + 1) * size] for i in range(4)]
            )
            total = pick(quarter_back[...], (skip[pair].astype(F32) + own).astype(BF16))
            out[2 * pair + 1] = total[:level_size]
            out[lax.rem(2 * pair + 2, depth)] = total[level_size:]
        return carry

    lax.fori_loop(0, pairs // TOGETHER, finish_coarse, 0)

    def drain(pair, carry):
        for phase in (phase_one, phase_two, phase_three, phase_four):
            for copy in phase(pair):
                copy.wait_send()
        return carry

    lax.fori_loop(0, pairs, drain, 0)


def body(
    lats, lons, field,
    a_norm_one, a_project, a_bias, a_output, a_norm_two, a_raise, a_lower,
    merge_norm_gain, merge_weight,
    b_norm_one, b_project, b_bias, b_output, b_norm_two, b_raise, b_lower,
    up_first, up_norm, up_second,
):
    depth, rows, columns, width = field.shape
    double = merge_weight.shape[1]
    pairs = depth // WIN_P
    size = WIN_P * WIN_LAT * WIN_LON
    fine, coarse = Grid(rows, columns), Grid(rows // 2, columns // 2)
    quarter = fine.quarters()

    def one_hot(matrix):
        return jnp.asarray(matrix.astype(BF16))

    fine_own, fine_halo = fine.gather()
    coarse_own, coarse_halo = coarse.gather()
    orders = [
        fine.send(), fine_own, fine_halo, fine_halo.T, quarter @ fine_own.T, quarter @ fine.send().T,
        quarter, quarter.T,
        coarse.send(), coarse_own, coarse_halo, coarse_halo.T, coarse_own.T, coarse.send().T,
    ]
    token = np.arange(size)
    level = token // (WIN_LAT * WIN_LON)
    edge = (token // WIN_LON) % WIN_LAT // HALF_LAT
    codes = np.zeros((3, size, GROUP), np.float32)
    for kind, flags in enumerate((level, edge)):
        codes[0, :, 2 * kind], codes[0, :, 2 * kind + 1] = flags, 1 - flags
        codes[kind + 1, :, 2 * kind], codes[kind + 1, :, 2 * kind + 1] = (
            EXCLUDED * (1 - flags), EXCLUDED * flags
        )
    operands = [
        field.reshape(depth, rows * columns, width),
        a_norm_one, a_project, a_bias.reshape(-1, size), a_output, a_norm_two,
        a_raise, a_lower.T,
        merge_norm_gain, merge_weight,
        b_norm_one, b_project, b_bias.reshape(-1, size), b_output, b_norm_two,
        b_raise, b_lower,
        up_first, up_norm, up_second,
    ]
    operands += [one_hot(matrix) for matrix in orders + [codes[0]]] + [jnp.asarray(code) for code in codes[1:]]
    vmem = pl.BlockSpec(memory_space=pltpu.VMEM)
    specs = [vmem] * len(operands)
    moved = [2, 3, 21, 22, 23, 24, 25, 26, 4, 6, 7, 9, 28, 29, 30, 11, 12, 31, 32, 33, 13, 15, 16, 17, 19, 27]
    for place in moved:
        specs[place] = pl.BlockSpec(memory_space=pl.ANY)
    wide = pl.cdiv(width, GROUP) * GROUP
    result = pl.pallas_call(
        functools.partial(section, fine, coarse, lats, lons, [len(operands)] + moved),
        out_shape=jax.ShapeDtypeStruct((depth, rows * columns, width), BF16),
        in_specs=specs,
        out_specs=vmem,
        scratch_shapes=[
            pltpu.VMEM((pairs, fine.local, width), BF16),
            pltpu.VMEM((pairs, fine.local, width), BF16),
            pltpu.VMEM((pairs, coarse.local, double), BF16),
            pltpu.VMEM((pairs, coarse.local, double), BF16),
            pltpu.VMEM((TOGETHER, fine.local, wide), BF16),
            pltpu.VMEM((TOGETHER, fine.local, wide), BF16),
            pltpu.VMEM((TOGETHER, fine.local, 2 * wide), BF16),
            pltpu.VMEM((pairs, fine.local, width), BF16),
            pltpu.VMEM((pairs, coarse.local, double), BF16),
            pltpu.VMEM((TOGETHER * coarse.local, double), BF16),
            pltpu.VMEM((TOGETHER * coarse.local, double), BF16),
            pltpu.VMEM((TOGETHER * coarse.local, 2 * double), BF16),
            pltpu.VMEM((TOGETHER * coarse.local, double), BF16),
            pltpu.VMEM((TOGETHER, fine.local, width), BF16),
            pltpu.VMEM((3, width, wide), BF16),
            pltpu.VMEM((a_bias.shape[0] * size, size), F32),
            pltpu.VMEM((b_bias.shape[0] * size, size), F32),
        ]
        + [pltpu.VMEM((pairs, fine.halo, width), BF16)] * 4
        + [pltpu.VMEM((pairs, coarse.halo, double), BF16)] * 4
        + [pltpu.SemaphoreType.DMA((4, pairs, 3)), pltpu.SemaphoreType.DMA((4, pairs, 3))]
        + [pltpu.SemaphoreType.DMA((len(moved),))]
        + [pltpu.VMEM(operands[place].shape, operands[place].dtype) for place in moved],
        compiler_params=pltpu.CompilerParams(
            collective_id=0, has_side_effects=True, vmem_limit_bytes=56 * 1024 * 1024
        ),
    )(*operands)
    return result.reshape(field.shape)


def solution(mesh):
    in_specs = (P(None, "lat", "lon", None),) + (P(),) * 19
    return jax.shard_map(
        functools.partial(body, mesh.shape["lat"], mesh.shape["lon"]),
        mesh=mesh,
        in_specs=in_specs,
        out_specs=P(None, "lat", "lon", None),
        check_vma=False,
    )
```
